32 devices in a mesh: fsdp: 8 (over z, y), ctx: 2 (over x), tp: 2 (over core).
Axes of the slice: x: 2, y: 2, z: 4, core: 2. Of those that a mesh axis runs over, the one named last changes fastest.
Arguments:
- tokens: bfloat16 [2, 8192, 768], P(None, ('fsdp', 'ctx')), may hold values from -6 to 6
- gain_attn: bfloat16 [768], P('fsdp'), may hold values from 0.099609375 to 1.8984375
- w_query: bfloat16 [768, 768], P('fsdp', 'tp'), may hold values from -0.21875 to 0.21875
- w_key: bfloat16 [768, 768], P('fsdp', 'tp'), may hold values from -0.21875 to 0.21875
- w_value: bfloat16 [768, 768], P('fsdp', 'tp'), may hold values from -0.21875 to 0.21875
- w_out: bfloat16 [768, 768], P('tp', 'fsdp'), may hold values from -6 to 6
- gain_ffn: bfloat16 [768], P('fsdp'), may hold values from 0.099609375 to 1.8984375
- w_gate: bfloat16 [768, 1152], P('fsdp', 'tp'), may hold values from -0.21875 to 0.21875
- w_up: bfloat16 [768, 1152], P('fsdp', 'tp'), may hold values from -0.21875 to 0.21875
- w_down: bfloat16 [1152, 768], P('tp', 'fsdp'), may hold values from -0.1875 to 0.1875
- cotangent: bfloat16 [2, 8192, 768], P(None, ('fsdp', 'ctx')), may hold values from -6 to 6
Outputs:
- output: bfloat16 [2, 8192, 768], P(None, ('fsdp', 'ctx'))
- grad_tokens: float32 [2, 8192, 768], P(None, ('fsdp', 'ctx'))
- grad_gain_attn: float32 [768], P('fsdp')
- grad_query: float32 [768, 768], P('fsdp', 'tp')
- grad_key: float32 [768, 768], P('fsdp', 'tp')
- grad_value: float32 [768, 768], P('fsdp', 'tp')
- grad_out: float32 [768, 768], P('tp', 'fsdp')
- grad_gain_ffn: float32 [768], P('fsdp')
- grad_gate: float32 [768, 1152], P('fsdp', 'tp')
- grad_up: float32 [768, 1152], P('fsdp', 'tp')
- grad_down: float32 [1152, 768], P('tp', 'fsdp')
The draws below stay inside these ranges and needn't reach their ends.
All inputs are finite; a program needn't handle non-finite values.
Results may differ from the reference program's by a relative error of at most 0.025.
Values may be sent and summed in bfloat16 or wider, within the bound.
A program may use at most 192 MiB of HBM per device.

```python
import jax
import jax.numpy as jnp
from jax import lax

D = 768
HEADS = 12
HD = 64
FF = 1152
SLOTS = 2
LEN = 1024
SEQS = 16
N_FSDP = 8


def spiked(entries, key, source, target, shards_of, factor):
    def block_of(dim):
        return (jnp.arange(entries.shape[dim]) // (entries.shape[dim] // shards_of)).reshape((-1,) + (1,) * (entries.ndim - 1 - dim))

    first = jax.random.permutation(key, shards_of)[block_of(target)]
    far = (block_of(target) + shards_of // 2) % shards_of
    return jnp.where((block_of(source) == first) | (block_of(source) == far), factor * entries, entries)


def steps_of(own_key, extent, shards, smallest, high):
    loudness = 1.0
    for dim, blocks in shards:
        draws = jax.random.uniform(jax.random.fold_in(jax.random.fold_in(own_key, 6), dim), (blocks,), jnp.float32, smallest / len(shards), high / len(shards))
        loudness = loudness * jnp.repeat(jnp.exp(draws), extent[dim] // blocks).reshape((-1,) + (1,) * (len(extent) - 1 - dim))
    return loudness


def normal_values(own_key, dims, deviation, bound, pieces=(), held_as=jnp.bfloat16):
    drawn = jax.random.normal(own_key, dims, jnp.float32) * deviation
    if len(pieces) > 0:
        drawn = steps_of(own_key, dims, pieces, -0.22, 0.18) * drawn
    return jnp.clip(drawn, min=-bound, max=bound).astype(held_as)


def heavy_noise(stream_key, shape, spread, bound, shards, heavy, kind=jnp.bfloat16):
    values = spread * jax.random.normal(stream_key, shape, jnp.float32)
    if shards:
        values = values * steps_of(stream_key, shape, shards, -0.22, 0.18)
    return jnp.clip(spiked(values, jax.random.fold_in(stream_key, 3), *heavy), -bound, bound).astype(kind)


def setup_inputs(seed: int = 0) -> dict:
    keys = jax.random.split(jax.random.key(seed), 12)
    return {
        "tokens": normal_values(keys[0], (SLOTS, N_FSDP * LEN, D), 1.0, 6.0, ((1, 16),)),
        "gain_attn": jnp.clip(1.0 + 0.18 * jax.random.normal(keys[1], (D,), jnp.float32), 0.099609375, 1.8984375).astype(jnp.bfloat16),
        "w_query": normal_values(keys[2], (D, D), D ** -0.5, 0.21875, ((0, 8), (1, 2))),
        "w_key": normal_values(keys[3], (D, D), D ** -0.5, 0.21875, ((0, 8), (1, 2))),
        "w_value": normal_values(keys[4], (D, D), D ** -0.5, 0.21875, ((0, 8), (1, 2))),
        "w_out": normal_values(keys[5], (D, D), 1.0, 6.0, ((0, 2), (1, 8))),
        "gain_ffn": jnp.clip(1.0 + 0.18 * jax.random.normal(keys[6], (D,), jnp.float32), 0.099609375, 1.8984375).astype(jnp.bfloat16),
        "w_gate": normal_values(keys[7], (D, FF), D ** -0.5, 0.21875, ((0, 8), (1, 2))),
        "w_up": normal_values(keys[8], (D, FF), D ** -0.5, 0.21875, ((0, 8), (1, 2))),
        "w_down": normal_values(keys[9], (FF, D), FF ** -0.5, 0.1875, ((0, 2), (1, 8))),
        "cotangent": heavy_noise(keys[10], (SLOTS, N_FSDP * LEN, D), 1.0, 6.0, ((1, 16),), (1, 2, 16, 2.0)),
    }


eps_norm = 1e-05
rope_base = 160000.0

@jax.custom_vjp
def low(v):
    return lax.optimization_barrier(v.astype(jnp.bfloat16)).astype(jnp.float32)

@jax.custom_vjp
def low_back(v):
    return v

def low_keep(v):
    return (low(v), None)

def low_pass(kept, grad):
    return (grad,)

def back_keep(v):
    return (v, None)

def back_low(kept, grad):
    return (low(grad),)
low.defvjp(low_keep, low_pass)
low_back.defvjp(back_keep, back_low)

def layer_norm(x):
    mean = lax.optimization_barrier(jnp.mean(x, axis=-1, keepdims=True))
    centred = x - mean
    var = lax.optimization_barrier(jnp.mean(centred * centred, axis=-1, keepdims=True))
    return centred * lax.rsqrt(var + eps_norm)

def matmul(a, b):
    return jnp.dot(a, b, precision=lax.Precision.HIGHEST, preferred_element_type=jnp.float32)

def rope_angles(length):
    position = jnp.arange(length, dtype=jnp.int32).astype(jnp.float32)
    inverse = 1.0 / rope_base ** (jnp.arange(0, HD, 2, dtype=jnp.int32).astype(jnp.float32) / HD)
    angle = position[:, None] * inverse[None, :]
    angle = jnp.concatenate([angle, angle], axis=-1)
    return (jnp.cos(angle), jnp.sin(angle))

def rotate(heads, cosine, sine):
    half = heads.shape[-1] // 2
    turned = jnp.concatenate([-heads[..., half:], heads[..., :half]], axis=-1)
    return heads * cosine[:, None, :] + turned * sine[:, None, :]

def layer(x, gain_attn, w_query, w_key, w_value, w_out, gain_ffn, w_gate, w_up, w_down):
    cosine, sine = rope_angles(LEN)
    scale = HD ** (-0.5)
    h1 = low(layer_norm(x) * gain_attn)
    query = low(rotate(low_back(matmul(h1, w_query)).reshape(LEN, HEADS, HD), cosine, sine))
    key = low(rotate(low_back(matmul(h1, w_key)).reshape(LEN, HEADS, HD), cosine, sine))
    value = low(low_back(matmul(h1, w_value))).reshape(LEN, HEADS, HD)
    scores = low_back(jnp.einsum('qhd,khd->hqk', query, key, precision=lax.Precision.HIGHEST) * scale)
    shifted = jnp.exp(scores - lax.optimization_barrier(jnp.max(scores, axis=-1, keepdims=True)))
    probs = low(shifted / lax.optimization_barrier(jnp.sum(shifted, axis=-1, keepdims=True)))
    attended = jnp.einsum('hqk,khd->qhd', probs, value, precision=lax.Precision.HIGHEST)
    attended = low(low_back(attended)).reshape(LEN, D)
    x2 = x + low_back(matmul(attended, w_out))
    h2 = low(layer_norm(x2) * gain_ffn)
    gate = low_back(matmul(h2, w_gate))
    up_part = low_back(matmul(h2, w_up))
    hidden = low(jax.nn.gelu(gate, approximate=False) * up_part)
    return x2 + low_back(matmul(hidden, w_down))

def reference(tokens, gain_attn, w_query, w_key, w_value, w_out, gain_ffn, w_gate, w_up, w_down, cotangent):
    weights = tuple((w.astype(jnp.float32) for w in (gain_attn, w_query, w_key, w_value, w_out, gain_ffn, w_gate, w_up, w_down)))
    inputs = tokens.astype(jnp.float32).reshape(SEQS, LEN, D)
    cotans = cotangent.astype(jnp.float32).reshape(SEQS, LEN, D)

    def one_sequence(totals, pair):
        x, grad_y = pair
        result, back = jax.vjp(layer, x, *weights)
        grads = back(grad_y)
        totals = tuple((t + g for t, g in zip(totals, grads[1:])))
        return (totals, (result.astype(jnp.bfloat16), grads[0]))
    zeros = tuple((jnp.zeros_like(w) for w in weights))
    totals, (outputs, grad_inputs) = lax.scan(one_sequence, zeros, (inputs, cotans))
    whole_shape = (SLOTS, N_FSDP * LEN, D)
    return (outputs.reshape(whole_shape), grad_inputs.reshape(whole_shape), totals[0], totals[1], totals[2], totals[3], totals[4], totals[5], totals[6], totals[7], totals[8])
```

```python
from functools import partial

import jax
import jax.numpy as jnp
import numpy as np
from jax import lax
from jax.experimental import pallas as pl
from jax.experimental.pallas import tpu as pltpu
from jax.sharding import PartitionSpec as P

HD = 64


eps_norm = 1e-05
rope_base = 160000.0


def layer_norm(x):
    mean = jnp.mean(x, axis=-1, keepdims=True)
    centred = x - mean
    var = jnp.mean(centred * centred, axis=-1, keepdims=True)
    rstd = lax.rsqrt(var + eps_norm)
    return (centred * rstd, rstd)


def norm_back(grad_normed, normed, rstd):
    first = jnp.mean(grad_normed, axis=-1, keepdims=True)
    second = jnp.mean(grad_normed * normed, axis=-1, keepdims=True)
    return rstd * (grad_normed - first - normed * second)


def rope_angles(first, count, width):
    position = (first + jnp.arange(count, dtype=jnp.int32)).astype(jnp.float32)
    inverse = 1.0 / rope_base ** (
        jnp.arange(0, width, 2, dtype=jnp.int32).astype(jnp.float32) / width
    )
    angle = position[:, None] * inverse[None, :]
    angle = jnp.concatenate([angle, angle], axis=-1)
    return (jnp.cos(angle), jnp.sin(angle))


def rotate(heads, cosine, sine, sign):
    half = heads.shape[-1] // 2
    turned = jnp.concatenate([-heads[..., half:], heads[..., :half]], axis=-1)
    return heads * cosine[:, None, :] + sign * turned * sine[:, None, :]


def matmul(a, b):
    return jnp.dot(a, b, preferred_element_type=jnp.float32)


def on_device_blocks(
    tokens, gain_attn, w_query, w_key, w_value, w_out, gain_ffn, w_gate, w_up, w_down, cotangent
):
    full = (
        lax.all_gather(gain_attn, "fsdp", axis=0, tiled=True),
        lax.all_gather(w_query, "fsdp", axis=0, tiled=True),
        lax.all_gather(w_key, "fsdp", axis=0, tiled=True),
        lax.all_gather(w_value, "fsdp", axis=0, tiled=True),
        lax.all_gather(w_out, "fsdp", axis=1, tiled=True),
        lax.all_gather(gain_ffn, "fsdp", axis=0, tiled=True),
        lax.all_gather(w_gate, "fsdp", axis=0, tiled=True),
        lax.all_gather(w_up, "fsdp", axis=0, tiled=True),
        lax.all_gather(w_down, "fsdp", axis=1, tiled=True),
    )
    gain_one = full[0].astype(jnp.float32)
    gain_two = full[5].astype(jnp.float32)
    slots = tokens.shape[0]
    rows = tokens.shape[1]
    model = tokens.shape[2]
    flat = slots * rows
    x = tokens.astype(jnp.float32).reshape(flat, model)
    width = full[1].shape[1]
    heads = width // HD
    scale = HD ** (-0.5)
    cosine, sine = rope_angles(lax.axis_index("ctx") * rows, rows, HD)
    normed_one, rstd_one = layer_norm(x)
    h_one = (normed_one * gain_one).astype(jnp.bfloat16)
    query = rotate(
        matmul(h_one, full[1]).reshape(slots, rows, heads, HD), cosine, sine, 1.0
    ).astype(jnp.bfloat16)
    key_flat = (
        rotate(matmul(h_one, full[2]).reshape(slots, rows, heads, HD), cosine, sine, 1.0)
        .astype(jnp.bfloat16)
        .reshape(slots, rows, width)
    )
    value_flat = matmul(h_one, full[3]).astype(jnp.bfloat16).reshape(slots, rows, width)
    piece = (
        lax.all_gather(key_flat, "ctx", axis=1, tiled=True),
        lax.all_gather(value_flat, "ctx", axis=1, tiled=True),
    )
    best = jnp.full((slots, heads, rows), -1e30, jnp.float32)
    keys = piece[0].reshape(slots, -1, heads, HD)
    values = piece[1].reshape(slots, -1, heads, HD)
    scores = jnp.einsum("bqhd,bkhd->bhqk", query, keys, preferred_element_type=jnp.float32) * scale
    newbest = jnp.maximum(best, jnp.max(scores, axis=-1))
    weights = jnp.exp(scores - newbest[..., None])
    total = jnp.sum(weights, axis=-1)
    accum = jnp.einsum(
        "bhqk,bkhd->bhqd", weights.astype(jnp.bfloat16), values, preferred_element_type=jnp.float32
    )
    best, total, accum = (newbest, total, accum)
    log_total = best + jnp.log(total)
    attended = (
        (accum / total[..., None]).transpose(0, 2, 1, 3).reshape(flat, width).astype(jnp.bfloat16)
    )
    x_two = x + lax.psum(matmul(attended, full[4]).astype(jnp.bfloat16), "tp").astype(jnp.float32)
    normed_two, rstd_two = layer_norm(x_two)
    h_two = (normed_two * gain_two).astype(jnp.bfloat16)
    gate = matmul(h_two, full[6])
    up_part = matmul(h_two, full[7])
    activated, gelu_back = jax.vjp(partial(jax.nn.gelu, approximate=False), gate)
    hidden = (activated * up_part).astype(jnp.bfloat16)
    result = x_two + lax.psum(matmul(hidden, full[8]).astype(jnp.bfloat16), "tp").astype(
        jnp.float32
    )
    output = result.astype(jnp.bfloat16).reshape(slots, rows, model)
    grad_y = cotangent.astype(jnp.float32).reshape(flat, model)
    grad_low = grad_y.astype(jnp.bfloat16)
    grad_hidden = matmul(grad_low, full[8].T)
    grad_down = matmul(hidden.T, grad_low)
    grad_gate_act = gelu_back(grad_hidden * up_part)[0].astype(jnp.bfloat16)
    grad_up_act = (grad_hidden * activated).astype(jnp.bfloat16)
    grad_gate = matmul(h_two.T, grad_gate_act)
    grad_up = matmul(h_two.T, grad_up_act)
    grad_h_two = lax.psum(
        (matmul(grad_gate_act, full[6].T) + matmul(grad_up_act, full[7].T)).astype(jnp.bfloat16),
        "tp",
    ).astype(jnp.float32)
    grad_gain_ffn = jnp.sum(grad_h_two * normed_two, axis=0)
    grad_x_two = grad_y + norm_back(grad_h_two * gain_two, normed_two, rstd_two)
    branch_low = grad_x_two.astype(jnp.bfloat16)
    grad_out = matmul(attended.T, branch_low)
    grad_att = matmul(branch_low, full[4].T).astype(jnp.bfloat16)
    delta_rows = jnp.sum(
        (grad_att.astype(jnp.float32) * attended.astype(jnp.float32)).reshape(
            slots, rows, heads, HD
        ),
        axis=-1,
    )
    delta = delta_rows.transpose(0, 2, 1)
    grad_att_heads = grad_att.reshape(slots, rows, heads, HD)
    stats_all = (
        lax.all_gather(log_total.transpose(0, 2, 1), "ctx", axis=1, tiled=True),
        lax.all_gather(delta_rows, "ctx", axis=1, tiled=True),
    )
    own_keys = key_flat.reshape(slots, rows, heads, HD)
    own_values = value_flat.reshape(slots, rows, heads, HD)
    piece = (
        lax.all_gather(query, "ctx", axis=1, tiled=True),
        lax.all_gather(grad_att_heads, "ctx", axis=1, tiled=True),
    )
    queries = piece[0]
    grads_in = piece[1]
    lse_piece = stats_all[0].transpose(0, 2, 1)
    delta_piece = stats_all[1].transpose(0, 2, 1)
    scores = (
        jnp.einsum("bqhd,bkhd->bhqk", queries, own_keys, preferred_element_type=jnp.float32) * scale
    )
    probs = jnp.exp(scores - lse_piece[..., None])
    grad_probs = jnp.einsum(
        "bqhd,bkhd->bhqk", grads_in, own_values, preferred_element_type=jnp.float32
    )
    grad_scores = (probs * (grad_probs - delta_piece[..., None])).astype(jnp.bfloat16)
    grad_keys_acc = (
        jnp.einsum("bhqk,bqhd->bkhd", grad_scores, queries, preferred_element_type=jnp.float32)
        * scale
    )
    grad_values_acc = jnp.einsum(
        "bhqk,bqhd->bkhd", probs.astype(jnp.bfloat16), grads_in, preferred_element_type=jnp.float32
    )
    piece = (
        lax.all_gather(key_flat, "ctx", axis=1, tiled=True),
        lax.all_gather(value_flat, "ctx", axis=1, tiled=True),
    )
    keys = piece[0].reshape(slots, -1, heads, HD)
    values = piece[1].reshape(slots, -1, heads, HD)
    scores = jnp.einsum("bqhd,bkhd->bhqk", query, keys, preferred_element_type=jnp.float32) * scale
    probs = jnp.exp(scores - log_total[..., None])
    grad_probs = jnp.einsum(
        "bqhd,bkhd->bhqk", grad_att_heads, values, preferred_element_type=jnp.float32
    )
    grad_scores = (probs * (grad_probs - delta[..., None])).astype(jnp.bfloat16)
    probs, grad_scores = (probs, grad_scores)
    grad_query_rot = (
        jnp.einsum("bhqk,bkhd->bqhd", grad_scores, keys, preferred_element_type=jnp.float32) * scale
    )
    grad_query_raw = (
        rotate(grad_query_rot, cosine, sine, -1.0).reshape(flat, width).astype(jnp.bfloat16)
    )
    grad_key_raw = (
        rotate(grad_keys_acc, cosine, sine, -1.0).reshape(flat, width).astype(jnp.bfloat16)
    )
    grad_value_raw = grad_values_acc.reshape(flat, width).astype(jnp.bfloat16)
    grad_query = matmul(h_one.T, grad_query_raw)
    grad_key = matmul(h_one.T, grad_key_raw)
    grad_value = matmul(h_one.T, grad_value_raw)
    grad_h_one = lax.psum(
        (
            matmul(grad_query_raw, full[1].T)
            + matmul(grad_key_raw, full[2].T)
            + matmul(grad_value_raw, full[3].T)
        ).astype(jnp.bfloat16),
        "tp",
    ).astype(jnp.float32)
    grad_gain_attn = jnp.sum(grad_h_one * normed_one, axis=0)
    grad_tokens = (grad_x_two + norm_back(grad_h_one * gain_one, normed_one, rstd_one)).reshape(
        slots, rows, model
    )
    pieces = (
        lax.psum_scatter(
            grad_gain_attn.astype(jnp.bfloat16), "fsdp", scatter_dimension=0, tiled=True
        ).astype(jnp.float32),
        lax.psum_scatter(
            grad_query.astype(jnp.bfloat16), "fsdp", scatter_dimension=0, tiled=True
        ).astype(jnp.float32),
        lax.psum_scatter(
            grad_key.astype(jnp.bfloat16), "fsdp", scatter_dimension=0, tiled=True
        ).astype(jnp.float32),
        lax.psum_scatter(
            grad_value.astype(jnp.bfloat16), "fsdp", scatter_dimension=0, tiled=True
        ).astype(jnp.float32),
        lax.psum_scatter(
            grad_out.astype(jnp.bfloat16), "fsdp", scatter_dimension=1, tiled=True
        ).astype(jnp.float32),
        lax.psum_scatter(
            grad_gain_ffn.astype(jnp.bfloat16), "fsdp", scatter_dimension=0, tiled=True
        ).astype(jnp.float32),
        lax.psum_scatter(
            grad_gate.astype(jnp.bfloat16), "fsdp", scatter_dimension=0, tiled=True
        ).astype(jnp.float32),
        lax.psum_scatter(
            grad_up.astype(jnp.bfloat16), "fsdp", scatter_dimension=0, tiled=True
        ).astype(jnp.float32),
        lax.psum_scatter(
            grad_down.astype(jnp.bfloat16), "fsdp", scatter_dimension=1, tiled=True
        ).astype(jnp.float32),
    )
    owned = (
        lax.psum(pieces[0].astype(jnp.bfloat16), "ctx").astype(jnp.float32),
        lax.psum(pieces[1].astype(jnp.bfloat16), "ctx").astype(jnp.float32),
        lax.psum(pieces[2].astype(jnp.bfloat16), "ctx").astype(jnp.float32),
        lax.psum(pieces[3].astype(jnp.bfloat16), "ctx").astype(jnp.float32),
        lax.psum(pieces[4].astype(jnp.bfloat16), "ctx").astype(jnp.float32),
        lax.psum(pieces[5].astype(jnp.bfloat16), "ctx").astype(jnp.float32),
        lax.psum(pieces[6].astype(jnp.bfloat16), "ctx").astype(jnp.float32),
        lax.psum(pieces[7].astype(jnp.bfloat16), "ctx").astype(jnp.float32),
        lax.psum(pieces[8].astype(jnp.bfloat16), "ctx").astype(jnp.float32),
    )
    return (
        output,
        grad_tokens,
        owned[0],
        owned[1],
        owned[2],
        owned[3],
        owned[4],
        owned[5],
        owned[6],
        owned[7],
        owned[8],
    )


swapped = ((0, 1), (1, 0))


MESH = pl.DeviceIdType.MESH


def greet(with_ctx):
    count = lax.axis_size("fsdp")
    me = lax.axis_index("fsdp")
    barrier = pltpu.get_barrier_semaphore()
    for step in range(1, count):
        there = lax.rem(me + step, count)
        pl.semaphore_signal(barrier, inc=1, device_id={"fsdp": there}, device_id_type=MESH)
    if with_ctx:
        there = 1 - lax.axis_index("ctx")
        pl.semaphore_signal(barrier, inc=1, device_id={"ctx": there}, device_id_type=MESH)
    pl.semaphore_wait(barrier, count - 1 + int(with_ctx))


def gather_copies(src, dst, send, recv, local):
    count = lax.axis_size("fsdp")
    me = lax.axis_index("fsdp")
    copies = [pltpu.make_async_copy(src, dst.at[me], local)]
    for step in range(1, count):
        copies.append(
            pltpu.make_async_remote_copy(
                src_ref=src,
                dst_ref=dst.at[me],
                send_sem=send.at[step - 1],
                recv_sem=recv.at[step - 1],
                device_id={"fsdp": lax.rem(me + step, count)},
                device_id_type=MESH,
            )
        )
    return copies


def scatter_copies(src, slots, send, recv, local):
    count = lax.axis_size("fsdp")
    me = lax.axis_index("fsdp")
    copies = [pltpu.make_async_copy(src.at[me], slots.at[0], local)]
    for step in range(1, count):
        there = lax.rem(me + step, count)
        copies.append(
            pltpu.make_async_remote_copy(
                src_ref=src.at[there],
                dst_ref=slots.at[step],
                send_sem=send.at[step - 1],
                recv_sem=recv.at[step - 1],
                device_id={"fsdp": there},
                device_id_type=MESH,
            )
        )
    return copies


def add_up(slots, low, other, out, send, recv):
    total = slots[0].astype(jnp.float32)
    for step in range(1, slots.shape[0]):
        total += slots[step].astype(jnp.float32)
    low[...] = total.astype(low.dtype)
    copy = pltpu.make_async_remote_copy(
        src_ref=low,
        dst_ref=other,
        send_sem=send,
        recv_sem=recv,
        device_id={"ctx": 1 - lax.axis_index("ctx")},
        device_id_type=MESH,
    )
    copy.start()
    return copy


def finish_sums(groups, ctx_send, ctx_recv):
    later = []
    for n, (slots, low, other, out) in enumerate(groups):
        later.append(add_up(slots, low, other, out, ctx_send.at[n], ctx_recv.at[n]))
    for copy, (slots, low, other, out) in zip(later, groups):
        copy.wait()
        out[...] = low[...].astype(jnp.float32) + other[...].astype(jnp.float32)


def semaphores(arrays, count):
    return [
        pltpu.SemaphoreType.DMA((arrays, count - 1)),
        pltpu.SemaphoreType.DMA((arrays, count - 1)),
        pltpu.SemaphoreType.DMA((arrays,)),
    ]


def sums_scratch(blocks):
    shapes = []
    for b in blocks:
        shapes += [pltpu.VMEM(b.shape, b.dtype)] + [pltpu.VMEM(b.shape[1:], b.dtype)] * 2
    many = len(blocks)
    return (
        shapes
        + semaphores(many, blocks[0].shape[0])
        + [pltpu.SemaphoreType.DMA((many,)), pltpu.SemaphoreType.DMA((many,))]
    )


def sums_parts(srcs, outs, scratch):
    many = len(srcs)
    send, recv, local, ctx_send, ctx_recv = scratch[3 * many :]
    copies, groups = [], []
    for n in range(many):
        slots, low, other = scratch[3 * n : 3 * n + 3]
        copies += scatter_copies(srcs[n], slots, send.at[n], recv.at[n], local.at[n])
        groups.append((slots, low, other, outs[n]))
    return copies, groups, ctx_send, ctx_recv


def scatter_kernel(*refs, many):
    greet(True)
    copies, groups, ctx_send, ctx_recv = sums_parts(
        refs[:many], refs[many : 2 * many], refs[2 * many :]
    )
    for copy in copies:
        copy.start()
    for copy in copies:
        copy.wait()
    finish_sums(groups, ctx_send, ctx_recv)


def scatter(*blocks):
    return pl.pallas_call(
        partial(scatter_kernel, many=len(blocks)),
        in_specs=[pl.BlockSpec(memory_space=pl.ANY)] * len(blocks),
        out_specs=[pl.BlockSpec(memory_space=pltpu.VMEM)] * len(blocks),
        out_shape=[jax.ShapeDtypeStruct(b.shape[1:], jnp.float32) for b in blocks],
        scratch_shapes=sums_scratch(blocks),
        compiler_params=pltpu.CompilerParams(
            collective_id=1, has_side_effects=True, vmem_limit_bytes=44 << 20
        ),
        name="scatter",
    )(*blocks)


def as_blocks(grad):
    return grad.astype(jnp.bfloat16).reshape(lax.axis_size("fsdp"), -1, grad.shape[1])


def sum_tp(part):
    part = part.astype(jnp.bfloat16)
    other = lax.ppermute(part, "tp", swapped)
    return part.astype(jnp.float32) + other.astype(jnp.float32)


def take_sequence(blocks):
    c = lax.axis_index("ctx")
    own = lax.dynamic_index_in_dim(blocks, c, 0, keepdims=False)
    give = lax.dynamic_index_in_dim(blocks, 1 - c, 0, keepdims=False)
    return jnp.concatenate([own, lax.ppermute(give, "ctx", swapped)], axis=0)


def give_back(own, came):
    c = lax.axis_index("ctx")
    return jnp.where(c == 0, jnp.stack([own, came]), jnp.stack([came, own]))


def dot(a, b, over):
    return lax.dot_general(a, b, (over, ((), ())), preferred_element_type=jnp.float32)


def turn(u):
    lane = lax.broadcasted_iota(jnp.int32, u.shape, 1)
    return jnp.where(lane % HD < HD // 2, -pltpu.roll(u, 96, 1), pltpu.roll(u, 32, 1))


def attend_back_kernel(*refs, tile):
    q_ref, k_ref, v_ref, o_ref, do_ref, lse_ref, cos_ref, sin_ref = refs[:8]
    out_ref = refs[11]
    dk_ref, dv_ref = refs[15:17]
    copies, groups, ctx_send, ctx_recv = sums_parts(refs[8:11], refs[12:15], refs[17:])

    @pl.when(pl.program_id(0) == 0)
    def _():
        greet(True)
        for copy in copies:
            copy.start()

    rows = q_ref.shape[0]
    k, v = k_ref[...], v_ref[...]
    k_turned = k.astype(jnp.float32).T.astype(jnp.bfloat16)
    lane = lax.broadcasted_iota(jnp.int32, (tile, 128), 1)
    dk_ref[...] = jnp.zeros_like(dk_ref)
    dv_ref[...] = jnp.zeros_like(dv_ref)
    for start in range(0, rows, tile):
        at = slice(start, start + tile)
        q = q_ref[at, :] * jnp.bfloat16(HD ** (-0.5))
        do = do_ref[at, :]
        prod = (do.astype(jnp.float32) * o_ref[at, :].astype(jnp.float32)).T
        outs = []
        for head in range(2):
            mine = (lane // HD) == head
            qm = jnp.where(mine, q, jnp.zeros_like(q))
            dm = jnp.where(mine, do, jnp.zeros_like(do))
            delta = jnp.sum(prod[head * HD : (head + 1) * HD], axis=0, keepdims=True)
            p = jnp.exp(dot(k, qm, ((1,), (1,))) - lse_ref[0, head : head + 1, at])
            ds = (p * (dot(v, dm, ((1,), (1,))) - delta)).astype(jnp.bfloat16)
            dv_ref[...] += dot(p.astype(jnp.bfloat16), dm, ((1,), (0,)))
            dk_ref[...] += dot(ds, qm, ((1,), (0,)))
            outs.append(dot(k_turned[head * HD : (head + 1) * HD], ds, ((1,), (0,))))
        dq = jnp.concatenate(outs, axis=0).T * (HD ** (-0.5))
        dq = dq * cos_ref[at, :] - turn(dq) * sin_ref[at, :]
        out_ref[at, :128] = dq.astype(jnp.bfloat16)
    dk = dk_ref[...]
    out_ref[:, 128:256] = (dk * cos_ref[...] - turn(dk) * sin_ref[...]).astype(jnp.bfloat16)
    out_ref[:, 256:] = dv_ref[...].astype(jnp.bfloat16)

    @pl.when(pl.program_id(0) == pl.num_programs(0) - 1)
    def _():
        for copy in copies:
            copy.wait()
        finish_sums(groups, ctx_send, ctx_recv)


def attend_back(q, k, v, o, do, lse, cosine, sine, *blocks):
    rows, width = q.shape
    pairs = width // 128
    column = pl.BlockSpec((rows, 128), lambda i: (0, i))
    table = pl.BlockSpec((rows, 128), lambda i: (0, 0))
    return pl.pallas_call(
        partial(attend_back_kernel, tile=min(512, rows)),
        grid=(pairs,),
        in_specs=[column] * 5
        + [pl.BlockSpec((1, 2, rows), lambda i: (i, 0, 0)), table, table]
        + [pl.BlockSpec(memory_space=pl.ANY)] * len(blocks),
        out_specs=[pl.BlockSpec((rows, 384), lambda i: (0, i))]
        + [pl.BlockSpec(b.shape[1:], lambda i: (0, 0)) for b in blocks],
        out_shape=[jax.ShapeDtypeStruct((rows, 3 * width), jnp.bfloat16)]
        + [jax.ShapeDtypeStruct(b.shape[1:], jnp.float32) for b in blocks],
        scratch_shapes=[pltpu.VMEM((rows, 128), jnp.float32)] * 2 + sums_scratch(blocks),
        compiler_params=pltpu.CompilerParams(
            collective_id=3, has_side_effects=True, vmem_limit_bytes=48 << 20
        ),
        cost_estimate=pl.CostEstimate(
            flops=30 * 10**9, bytes_accessed=10**7, transcendentals=pairs * 2 * rows * rows
        ),
        name="attend_back",
    )(q, k, v, o, do, lse, cosine, sine, *blocks)


def rope_tables(rows):
    angle = np.arange(2 * rows, dtype=np.float32)[:, None] * (
        np.float32(1.0)
        / np.float32(rope_base) ** (np.arange(0, HD, 2, dtype=np.float32) / np.float32(HD))
    )[None, :].astype(np.float32)
    tables = []
    for values in (np.cos(angle), np.sin(angle)):
        whole = jnp.asarray(np.tile(values.astype(np.float32), (1, 4)))
        flipped = jnp.concatenate([whole[rows:], whole[:rows]], axis=0)
        tables.append(jnp.where(lax.axis_index("ctx") == 0, whole, flipped))
    return tables


def remote(src, dst, send, recv, to):
    return pltpu.make_async_remote_copy(
        src_ref=src, dst_ref=dst, send_sem=send, recv_sem=recv, device_id=to, device_id_type=MESH
    )


def position():
    f = lax.axis_index("fsdp")
    return f, f // 2, lax.rem(f, 2), lax.axis_index("ctx"), lax.axis_index("tp")


def greet_all(peers):
    barrier = pltpu.get_barrier_semaphore()
    for peer in peers:
        pl.semaphore_signal(barrier, inc=1, device_id=peer, device_id_type=MESH)
    pl.semaphore_wait(barrier, len(peers))


class Gather:
    def __init__(self, buf, send, recv, half):
        f, z, y, c, _ = position()
        rows = buf.shape[1]
        part = pl.ds(0, rows)
        if half:
            part = pl.ds(pl.multiple_of(c * (rows // 2), 16), rows // 2)

        def hop(slot, n, to):
            ref = buf.at[slot, part]
            return remote(ref, ref, send.at[n], recv.at[n], to)

        across = z * 2 + 1 - y
        came = [lax.rem(z + 3 - k, 4) * 2 + y for k in range(3)]
        far = [lax.rem(z + 3 - k, 4) * 2 + 1 - y for k in range(3)]
        over_y, over_x = {"fsdp": across}, {"ctx": 1 - c}
        self.along = [hop(f, k, {"fsdp": lax.rem(z + k + 1, 4) * 2 + y}) for k in range(3)]
        self.own_y = hop(f, 3, over_y)
        self.next_y = [hop(came[k], 4 + k, over_y) for k in range(3)]
        self.half = half
        if half:
            self.own_x = hop(across, 7, over_x)
            self.next_x = [hop(came[k], 8 + k, over_x) for k in range(3)]
            self.last_x = [hop(far[k], 11 + k, over_x) for k in range(3)]

    def begin(self):
        self.along[0].start()
        self.own_y.start()
        self.along[1].start()
        self.along[2].start()

    def middle(self):
        if self.half:
            self.own_y.wait_recv()
            self.own_x.start()
        for k in range(3):
            self.along[k].wait_recv()
            self.next_y[k].start()
            if self.half:
                self.next_x[k].start()

    def late(self):
        if self.half:
            for k in range(3):
                self.next_y[k].wait_recv()
                self.last_x[k].start()

    def ready(self):
        if self.half:
            for copy in [self.own_x] + self.next_x + self.last_x:
                copy.wait_recv()
        else:
            for copy in [self.own_y] + self.next_y:
                copy.wait_recv()

    def finish(self):
        copies = self.along + [self.own_y] + self.next_y
        if self.half:
            copies = copies + [self.own_x] + self.next_x + self.last_x
        for copy in copies:
            copy.wait_send()


class Swap:
    def __init__(self, src, dst, send, recv):
        _, _, _, c, t = position()
        rows = dst.shape[0] // 2
        part = pl.ds(pl.multiple_of(t * rows, 16), rows)
        self.over_x = remote(src.at[part], dst.at[part], send.at[0], recv.at[0], {"ctx": 1 - c})
        self.over = remote(dst.at[part], dst.at[part], send.at[1], recv.at[1], {"tp": 1 - t})

    def begin(self):
        self.over_x.start()

    def middle(self):
        self.over_x.wait_recv()
        self.over.start()

    def ready(self):
        self.over.wait_recv()

    def finish(self):
        self.over_x.wait_send()
        self.over.wait_send()


class TwoCores:
    def __init__(self, own, other, send, recv, chunk):
        t = lax.axis_index("tp")
        self.own, self.other, self.chunk = own, other, chunk
        self.copies = []
        for n in range(own.shape[0] // chunk):
            at = pl.ds(n * chunk, chunk)
            self.copies.append(
                remote(own.at[at], other.at[at], send.at[n], recv.at[n], {"tp": 1 - t})
            )

    def give(self, n, part):
        self.own[n * self.chunk : (n + 1) * self.chunk, :] = part.astype(jnp.bfloat16)
        self.copies[n].start()

    def take(self, n):
        at = slice(n * self.chunk, (n + 1) * self.chunk)
        self.copies[n].wait_recv()
        return self.own[at, :].astype(jnp.float32) + self.other[at, :].astype(jnp.float32)

    def finish(self):
        for copy in self.copies:
            copy.wait_send()


def place_matrix(n, part, model):
    row = lax.broadcasted_iota(jnp.int32, (128, model), 0)
    col = lax.broadcasted_iota(jnp.int32, (128, model), 1)
    return jnp.where((col == row + n * part) & (row < part), 1.0, 0.0)


CHUNK = 256


def forward_kernel(*refs, part, tile):
    tok, cot, gains, wq, wk, wv, wo, wgu, wd, cos_ref, sin_ref = refs[:11]
    outs = refs[11:31]
    (came, cotcame, gbuf, gain, h1, q, k, v, o, lse, x2, h2, hid, upf, act, wqkv, wob, wgub, wdb, y) = refs[31:51]
    pa, oa, pb, ob, gsend, grecv, wsend, wrecv, ssend, srecv, tsend, trecv, osem = refs[51:]
    f, z, yy, c, t = position()
    count = 8
    model = h1.shape[1]
    rows = h1.shape[0]
    half = rows // 2
    width = q.shape[1]
    pairs = width // 128
    units = hid.shape[1]
    chunks = rows // CHUNK

    for p in range(pairs):
        at = slice(p * 128, (p + 1) * 128)
        wqkv[p, f, :, 0:128] = wq[:, at]
        wqkv[p, f, :, 128:256] = wk[:, at]
        wqkv[p, f, :, 256:384] = wv[:, at]
    gbuf[f] = gains[...]
    greet_all(
        [{"fsdp": lax.rem(f + n, count)} for n in range(1, count)]
        + [{"ctx": 1 - c}, {"tp": 1 - t}]
    )
    gain_copies = [
        remote(gbuf.at[f], gbuf.at[f], gsend.at[n - 1], grecv.at[n - 1], {"fsdp": lax.rem(f + n, count)})
        for n in range(1, count)
    ]
    for copy in gain_copies:
        copy.start()
    pieces = []
    for n in range(pairs):
        pieces.append(Gather(wqkv.at[n], wsend.at[n], wrecv.at[n], HALF[n]))
    for n, buf in enumerate((wob, wgub, wdb)):
        n += pairs
        pieces.append(Gather(buf, wsend.at[n], wrecv.at[n], HALF[n]))
    tokens = Swap(tok.at[1 - c], came, ssend.at[0], srecv.at[0])
    cotan = Swap(cot.at[1 - c], cotcame, ssend.at[1], srecv.at[1])
    a0, a1, a2, b0, b1, b2 = pieces
    a0.begin()
    tokens.begin()
    a1.begin()
    wob[f] = wo[...]
    wgub[f] = wgu[...]
    wdb[f] = wd[...]

    for n in range(half // CHUNK):
        at = slice(n * CHUNK, (n + 1) * CHUNK)
        x2[at, :] = layer_norm(tok[c, at, :].astype(jnp.float32))[0]
    a0.middle()
    a2.begin()
    for copy in gain_copies:
        copy.wait_recv()
    total = jnp.zeros((8, model), jnp.float32)
    for n in range(count):
        total += jnp.dot(gbuf[n], place_matrix(n, part, model), preferred_element_type=jnp.float32)
    gain[...] = total
    gain_one, gain_two = total[0:1], total[1:2]
    for n in range(half // CHUNK):
        at = slice(n * CHUNK, (n + 1) * CHUNK)
        h1[at, :] = (x2[at, :] * gain_one).astype(jnp.bfloat16)
    tokens.middle()
    a0.late()
    a1.middle()
    b0.begin()
    tokens.ready()
    cotan.begin()
    for n in range(half // CHUNK):
        at = slice(n * CHUNK, (n + 1) * CHUNK)
        there = slice(half + n * CHUNK, half + (n + 1) * CHUNK)
        h1[there, :] = (layer_norm(came[at, :].astype(jnp.float32))[0] * gain_one).astype(jnp.bfloat16)
    a0.ready()

    out_copies = []

    def emit(n, ref):
        copy = pltpu.make_async_copy(ref, outs[n], osem.at[n])
        copy.start()
        out_copies.append(copy)

    emit(0, came)
    emit(2, gbuf)
    emit(3, gain)
    emit(4, h1)

    def attend_pair(p, between):
        cols = slice(p * 128, (p + 1) * 128)
        w = wqkv[p].reshape(model, 384)
        lane = lax.broadcasted_iota(jnp.int32, (tile, 128), 1)
        for start in range(0, rows, tile):
            at = slice(start, start + tile)
            raw = jnp.dot(h1[at, :], w, preferred_element_type=jnp.float32)
            cosine, sine = cos_ref[at, :], sin_ref[at, :]
            q_raw, k_raw = raw[:, :128], raw[:, 128:256]
            q[at, cols] = (q_raw * cosine + turn(q_raw) * sine).astype(jnp.bfloat16)
            k[at, cols] = (k_raw * cosine + turn(k_raw) * sine).astype(jnp.bfloat16)
            v[at, cols] = raw[:, 256:].astype(jnp.bfloat16)
        v_turned = v[:, cols].astype(jnp.float32).T.astype(jnp.bfloat16)
        keys = k[:, cols]
        for n, start in enumerate(range(0, rows, tile)):
            at = slice(start, start + tile)
            query = q[at, cols] * jnp.bfloat16(HD ** (-0.5))
            heads = []
            for head in range(2):
                mine = (lane // HD) == head
                qm = jnp.where(mine, query, jnp.zeros_like(query))
                s = dot(keys, qm, ((1,), (1,)))
                top = jnp.max(s, axis=0, keepdims=True)
                e = jnp.exp(s - top)
                total = jnp.sum(e, axis=0, keepdims=True)
                lse[p, head : head + 1, at] = top + jnp.log(total)
                vh = v_turned[head * HD : (head + 1) * HD]
                heads.append(dot(vh, e.astype(jnp.bfloat16), ((1,), (0,))) / total)
            o[at, cols] = jnp.concatenate(heads, axis=0).T.astype(jnp.bfloat16)
            between[n]()

    def after_0():
        a1.late()
        a2.middle()
        b1.begin()

    def after_1():
        a2.late()
        b0.middle()
        cotan.middle()

    attend_pair(0, [after_0, lambda: None])
    a1.ready()
    attend_pair(1, [after_1, lambda: None])
    a2.ready()
    attend_pair(2, [lambda: (b0.late(), b1.middle(), b2.begin()), lambda: None])
    emit(5, q)
    emit(6, k)
    emit(7, v)
    emit(8, o)
    emit(9, lse)
    emit(15, wqkv)

    b0.ready()
    sum_one = TwoCores(pa, oa, tsend.at[0], trecv.at[0], CHUNK)
    sum_two = TwoCores(pb, ob, tsend.at[1], trecv.at[1], CHUNK)
    w = wob[...].reshape(model, width)
    for n in range(chunks):
        sum_one.give(n, dot(o[n * CHUNK : (n + 1) * CHUNK, :], w, ((1,), (1,))))
    b1.late()
    cotan.ready()
    emit(1, cotcame)
    emit(16, wob)
    for n in range(chunks):
        at = slice(n * CHUNK, (n + 1) * CHUNK)
        if n < chunks // 2:
            x = tok[c, at, :]
        else:
            x = came[n * CHUNK - half : (n + 1) * CHUNK - half, :]
        xx = x.astype(jnp.float32) + sum_one.take(n)
        x2[at, :] = xx
        h2[at, :] = (layer_norm(xx)[0] * gain_two).astype(jnp.bfloat16)
    emit(10, x2)
    emit(11, h2)
    b2.middle()
    b1.ready()
    w = wgub[...].reshape(model, 2 * units)
    for n in range(chunks):
        at = slice(n * CHUNK, (n + 1) * CHUNK)
        both = jnp.dot(h2[at, :], w, preferred_element_type=jnp.float32)
        gate, up = both[:, :units], both[:, units:]
        phi = 0.5 + 0.5 * lax.erf(gate * (0.5 ** 0.5))
        active = gate * phi
        slope = phi + gate * (jnp.exp(-0.5 * gate * gate) * (1.0 / (2.0 * np.pi) ** 0.5))
        hid[at, :] = (active * up).astype(jnp.bfloat16)
        upf[at, :] = (slope * up).astype(jnp.bfloat16)
        act[at, :] = active.astype(jnp.bfloat16)
        if n == 0:
            b2.late()
    b2.ready()
    emit(12, hid)
    emit(13, upf)
    emit(14, act)
    emit(17, wgub)
    emit(18, wdb)
    w = wdb[...].reshape(model, units)
    for n in range(chunks):
        sum_two.give(n, dot(hid[n * CHUNK : (n + 1) * CHUNK, :], w, ((1,), (1,))))
    for n in range(chunks):
        at = slice(n * CHUNK, (n + 1) * CHUNK)
        y[at, :] = (x2[at, :] + sum_two.take(n)).astype(jnp.bfloat16)
    emit(19, y)
    for piece in pieces + [tokens, cotan, sum_one, sum_two]:
        piece.finish()
    for copy in gain_copies:
        copy.wait_send()
    for copy in out_copies:
        copy.wait()


HALF = (False, False, True, False, True, True)


def forward(tokens, cotangent, gains, wq, wk, wv, wo, wgu, wd, cosine, sine):
    slots, half, model = tokens.shape
    rows = 2 * half
    part, width = wq.shape
    units = wd.shape[1]
    pairs = width // 128
    low, full = jnp.bfloat16, jnp.float32
    held = [
        ((half, model), low),
        ((half, model), low),
        ((8, 8, 128), full),
        ((8, model), full),
        ((rows, model), low),
        ((rows, width), low),
        ((rows, width), low),
        ((rows, width), low),
        ((rows, width), low),
        ((pairs, 2, rows), full),
        ((rows, model), full),
        ((rows, model), low),
        ((rows, units), low),
        ((rows, units), low),
        ((rows, units), low),
        ((pairs, 8, part, 384), low),
        ((8, part, width), low),
        ((8, part, 2 * units), low),
        ((8, part, units), low),
        ((rows, model), low),
    ]
    dma = pltpu.SemaphoreType.DMA
    return pl.pallas_call(
        partial(forward_kernel, part=part, tile=min(512, rows)),
        in_specs=[pl.BlockSpec(memory_space=pltpu.VMEM)] * 11,
        out_specs=[pl.BlockSpec(memory_space=pl.ANY)] * 20,
        out_shape=[jax.ShapeDtypeStruct(s, d) for s, d in held],
        scratch_shapes=[pltpu.VMEM(s, d) for s, d in held]
        + [pltpu.VMEM((rows, model), low)] * 4
        + [dma((7,)), dma((7,)), dma((6, 14)), dma((6, 14)), dma((2, 2)), dma((2, 2))]
        + [dma((2, rows // CHUNK)), dma((2, rows // CHUNK)), dma((20,))],
        compiler_params=pltpu.CompilerParams(
            collective_id=2, has_side_effects=True, vmem_limit_bytes=56 << 20
        ),
        name="forward",
    )(tokens, cotangent, gains, wq, wk, wv, wo, wgu, wd, cosine, sine)


def on_device(
    tokens, gain_attn, w_query, w_key, w_value, w_out, gain_ffn, w_gate, w_up, w_down, cotangent
):
    slots, rows, model = tokens.shape
    part = w_query.shape[0]
    width = w_query.shape[1]
    pairs = width // 128
    units = w_gate.shape[1]
    gains = jnp.pad(
        jnp.stack([gain_attn, gain_ffn]).astype(jnp.float32), ((0, 6), (0, 128 - part))
    )
    cosine, sine = rope_tables(rows)
    came, cotcame, _, gain, h_one, q, k, v, attended, lse, x_two, h_two, hidden, upf, act, qkv_w, out_w, ffn_w, down_w, y = forward(
        tokens, cotangent, gains, w_query, w_key, w_value, w_out.T,
        jnp.concatenate([w_gate, w_up], axis=1), w_down.T, cosine, sine,
    )
    gain_one, gain_two = gain[0], gain[1]
    c = lax.axis_index("ctx")
    x = jnp.concatenate([lax.dynamic_index_in_dim(tokens, c, 0, keepdims=False), came]).astype(jnp.float32)
    grad_low = jnp.concatenate([lax.dynamic_index_in_dim(cotangent, c, 0, keepdims=False), cotcame])
    grad_y = grad_low.astype(jnp.float32)
    normed_one, rstd_one = layer_norm(x)
    normed_two, rstd_two = layer_norm(x_two)
    out_w = out_w.reshape(model, width)
    ffn_w = ffn_w.reshape(model, 2 * units)
    down_w = down_w.reshape(model, units)
    qkv_w = qkv_w.reshape(pairs, model, 384).transpose(1, 0, 2).reshape(model, 3 * width)
    output = give_back(y[:rows], lax.ppermute(y[rows:], "ctx", swapped))

    grad_hidden = matmul(grad_low, down_w)
    grad_both = jnp.concatenate(
        [
            (grad_hidden * upf.astype(jnp.float32)).astype(jnp.bfloat16),
            (grad_hidden * act.astype(jnp.float32)).astype(jnp.bfloat16),
        ],
        axis=1,
    )
    grad_h_two = sum_tp(dot(grad_both, ffn_w, ((1,), (1,))))
    ffn_blocks = as_blocks(dot(h_two, grad_both, ((0,), (0,))))
    down_blocks = as_blocks(dot(grad_low, hidden, ((0,), (0,))))
    grad_gain_ffn = jnp.sum(grad_h_two * normed_two, axis=0)
    grad_x_two = grad_y + norm_back(grad_h_two * gain_two, normed_two, rstd_two)
    branch_low = grad_x_two.astype(jnp.bfloat16)
    out_blocks = as_blocks(dot(branch_low, attended, ((0,), (0,))))
    grad_att = matmul(branch_low, out_w).astype(jnp.bfloat16)
    grad_qkv, own_ffn, own_down, own_out = attend_back(
        q, k, v, attended, grad_att, lse, cosine, sine, ffn_blocks, down_blocks, out_blocks
    )
    grad_h_one = sum_tp(dot(grad_qkv, qkv_w, ((1,), (1,))))
    qkv_blocks = as_blocks(dot(h_one, grad_qkv, ((0,), (0,))))
    grad_gain_attn = jnp.sum(grad_h_one * normed_one, axis=0)
    grad_x = grad_x_two + norm_back(grad_h_one * gain_one, normed_one, rstd_one)
    came = lax.ppermute(grad_x[rows:].astype(jnp.bfloat16), "ctx", swapped).astype(jnp.float32)
    grad_tokens = give_back(grad_x[:rows], came)
    gain_blocks = jnp.pad(
        jnp.stack([grad_gain_attn, grad_gain_ffn]).reshape(2, -1, part).transpose(1, 0, 2),
        ((0, 0), (0, 6), (0, 128 - part)),
    )
    own_qkv, own_gains = scatter(qkv_blocks, gain_blocks)
    own_gains = own_gains[:, :part]
    own_qkv = own_qkv.reshape(part, pairs, 3, 128)
    return (
        output,
        grad_tokens,
        own_gains[0],
        own_qkv[:, :, 0].reshape(part, width),
        own_qkv[:, :, 1].reshape(part, width),
        own_qkv[:, :, 2].reshape(part, width),
        own_out.T,
        own_gains[1],
        own_ffn[:, :units],
        own_ffn[:, units:],
        own_down.T,
    )


def solution(mesh):
    whole = mesh.shape["ctx"] == 2 and mesh.shape["tp"] == 2
    step = on_device if whole and mesh.shape["fsdp"] == 8 else on_device_blocks
    placed = (
        P(None, ("fsdp", "ctx"), None),
        P("fsdp"),
        P("fsdp", "tp"),
        P("fsdp", "tp"),
        P("fsdp", "tp"),
        P("tp", "fsdp"),
        P("fsdp"),
        P("fsdp", "tp"),
        P("fsdp", "tp"),
        P("tp", "fsdp"),
        P(None, ("fsdp", "ctx"), None),
    )
    return jax.shard_map(
        step,
        mesh=mesh,
        in_specs=placed,
        out_specs=(
            P(None, ("fsdp", "ctx"), None),
            P(None, ("fsdp", "ctx"), None),
            P("fsdp"),
            P("fsdp", "tp"),
            P("fsdp", "tp"),
            P("fsdp", "tp"),
            P("tp", "fsdp"),
            P("fsdp"),
            P("fsdp", "tp"),
            P("fsdp", "tp"),
            P("tp", "fsdp"),
        ),
        check_vma=False,
    )
```

```python
from functools import partial

import jax
import jax.numpy as jnp
import numpy as np
from jax import lax
from jax.experimental import pallas as pl
from jax.experimental.pallas import tpu as pltpu
from jax.sharding import PartitionSpec as P

HD = 64


eps_norm = 1e-05
rope_base = 160000.0


def layer_norm(x):
    mean = jnp.mean(x, axis=-1, keepdims=True)
    centred = x - mean
    var = jnp.mean(centred * centred, axis=-1, keepdims=True)
    rstd = lax.rsqrt(var + eps_norm)
    return (centred * rstd, rstd)


def norm_back(grad_normed, normed, rstd):
    first = jnp.mean(grad_normed, axis=-1, keepdims=True)
    second = jnp.mean(grad_normed * normed, axis=-1, keepdims=True)
    return rstd * (grad_normed - first - normed * second)


def rope_angles(first, count, width):
    position = (first + jnp.arange(count, dtype=jnp.int32)).astype(jnp.float32)
    inverse = 1.0 / rope_base ** (
        jnp.arange(0, width, 2, dtype=jnp.int32).astype(jnp.float32) / width
    )
    angle = position[:, None] * inverse[None, :]
    angle = jnp.concatenate([angle, angle], axis=-1)
    return (jnp.cos(angle), jnp.sin(angle))


def rotate(heads, cosine, sine, sign):
    half = heads.shape[-1] // 2
    turned = jnp.concatenate([-heads[..., half:], heads[..., :half]], axis=-1)
    return heads * cosine[:, None, :] + sign * turned * sine[:, None, :]


def matmul(a, b):
    return jnp.dot(a, b, preferred_element_type=jnp.float32)


def on_device_blocks(
    tokens, gain_attn, w_query, w_key, w_value, w_out, gain_ffn, w_gate, w_up, w_down, cotangent
):
    full = (
        lax.all_gather(gain_attn, "fsdp", axis=0, tiled=True),
        lax.all_gather(w_query, "fsdp", axis=0, tiled=True),
        lax.all_gather(w_key, "fsdp", axis=0, tiled=True),
        lax.all_gather(w_value, "fsdp", axis=0, tiled=True),
        lax.all_gather(w_out, "fsdp", axis=1, tiled=True),
        lax.all_gather(gain_ffn, "fsdp", axis=0, tiled=True),
        lax.all_gather(w_gate, "fsdp", axis=0, tiled=True),
        lax.all_gather(w_up, "fsdp", axis=0, tiled=True),
        lax.all_gather(w_down, "fsdp", axis=1, tiled=True),
    )
    gain_one = full[0].astype(jnp.float32)
    gain_two = full[5].astype(jnp.float32)
    slots = tokens.shape[0]
    rows = tokens.shape[1]
    model = tokens.shape[2]
    flat = slots * rows
    x = tokens.astype(jnp.float32).reshape(flat, model)
    width = full[1].shape[1]
    heads = width // HD
    scale = HD ** (-0.5)
    cosine, sine = rope_angles(lax.axis_index("ctx") * rows, rows, HD)
    normed_one, rstd_one = layer_norm(x)
    h_one = (normed_one * gain_one).astype(jnp.bfloat16)
    query = rotate(
        matmul(h_one, full[1]).reshape(slots, rows, heads, HD), cosine, sine, 1.0
    ).astype(jnp.bfloat16)
    key_flat = (
        rotate(matmul(h_one, full[2]).reshape(slots, rows, heads, HD), cosine, sine, 1.0)
        .astype(jnp.bfloat16)
        .reshape(slots, rows, width)
    )
    value_flat = matmul(h_one, full[3]).astype(jnp.bfloat16).reshape(slots, rows, width)
    piece = (
        lax.all_gather(key_flat, "ctx", axis=1, tiled=True),
        lax.all_gather(value_flat, "ctx", axis=1, tiled=True),
    )
    best = jnp.full((slots, heads, rows), -1e30, jnp.float32)
    keys = piece[0].reshape(slots, -1, heads, HD)
    values = piece[1].reshape(slots, -1, heads, HD)
    scores = jnp.einsum("bqhd,bkhd->bhqk", query, keys, preferred_element_type=jnp.float32) * scale
    newbest = jnp.maximum(best, jnp.max(scores, axis=-1))
    weights = jnp.exp(scores - newbest[..., None])
    total = jnp.sum(weights, axis=-1)
    accum = jnp.einsum(
        "bhqk,bkhd->bhqd", weights.astype(jnp.bfloat16), values, preferred_element_type=jnp.float32
    )
    best, total, accum = (newbest, total, accum)
    log_total = best + jnp.log(total)
    attended = (
        (accum / total[..., None]).transpose(0, 2, 1, 3).reshape(flat, width).astype(jnp.bfloat16)
    )
    x_two = x + lax.psum(matmul(attended, full[4]).astype(jnp.bfloat16), "tp").astype(jnp.float32)
    normed_two, rstd_two = layer_norm(x_two)
    h_two = (normed_two * gain_two).astype(jnp.bfloat16)
    gate = matmul(h_two, full[6])
    up_part = matmul(h_two, full[7])
    activated, gelu_back = jax.vjp(partial(jax.nn.gelu, approximate=False), gate)
    hidden = (activated * up_part).astype(jnp.bfloat16)
    result = x_two + lax.psum(matmul(hidden, full[8]).astype(jnp.bfloat16), "tp").astype(
        jnp.float32
    )
    output = result.astype(jnp.bfloat16).reshape(slots, rows, model)
    grad_y = cotangent.astype(jnp.float32).reshape(flat, model)
    grad_low = grad_y.astype(jnp.bfloat16)
    grad_hidden = matmul(grad_low, full[8].T)
    grad_down = matmul(hidden.T, grad_low)
    grad_gate_act = gelu_back(grad_hidden * up_part)[0].astype(jnp.bfloat16)
    grad_up_act = (grad_hidden * activated).astype(jnp.bfloat16)
    grad_gate = matmul(h_two.T, grad_gate_act)
    grad_up = matmul(h_two.T, grad_up_act)
    grad_h_two = lax.psum(
        (matmul(grad_gate_act, full[6].T) + matmul(grad_up_act, full[7].T)).astype(jnp.bfloat16),
        "tp",
    ).astype(jnp.float32)
    grad_gain_ffn = jnp.sum(grad_h_two * normed_two, axis=0)
    grad_x_two = grad_y + norm_back(grad_h_two * gain_two, normed_two, rstd_two)
    branch_low = grad_x_two.astype(jnp.bfloat16)
    grad_out = matmul(attended.T, branch_low)
    grad_att = matmul(branch_low, full[4].T).astype(jnp.bfloat16)
    delta_rows = jnp.sum(
        (grad_att.astype(jnp.float32) * attended.astype(jnp.float32)).reshape(
            slots, rows, heads, HD
        ),
        axis=-1,
    )
    delta = delta_rows.transpose(0, 2, 1)
    grad_att_heads = grad_att.reshape(slots, rows, heads, HD)
    stats_all = (
        lax.all_gather(log_total.transpose(0, 2, 1), "ctx", axis=1, tiled=True),
        lax.all_gather(delta_rows, "ctx", axis=1, tiled=True),
    )
    own_keys = key_flat.reshape(slots, rows, heads, HD)
    own_values = value_flat.reshape(slots, rows, heads, HD)
    piece = (
        lax.all_gather(query, "ctx", axis=1, tiled=True),
        lax.all_gather(grad_att_heads, "ctx", axis=1, tiled=True),
    )
    queries = piece[0]
    grads_in = piece[1]
    lse_piece = stats_all[0].transpose(0, 2, 1)
    delta_piece = stats_all[1].transpose(0, 2, 1)
    scores = (
        jnp.einsum("bqhd,bkhd->bhqk", queries, own_keys, preferred_element_type=jnp.float32) * scale
    )
    probs = jnp.exp(scores - lse_piece[..., None])
    grad_probs = jnp.einsum(
        "bqhd,bkhd->bhqk", grads_in, own_values, preferred_element_type=jnp.float32
    )
    grad_scores = (probs * (grad_probs - delta_piece[..., None])).astype(jnp.bfloat16)
    grad_keys_acc = (
        jnp.einsum("bhqk,bqhd->bkhd", grad_scores, queries, preferred_element_type=jnp.float32)
        * scale
    )
    grad_values_acc = jnp.einsum(
        "bhqk,bqhd->bkhd", probs.astype(jnp.bfloat16), grads_in, preferred_element_type=jnp.float32
    )
    piece = (
        lax.all_gather(key_flat, "ctx", axis=1, tiled=True),
        lax.all_gather(value_flat, "ctx", axis=1, tiled=True),
    )
    keys = piece[0].reshape(slots, -1, heads, HD)
    values = piece[1].reshape(slots, -1, heads, HD)
    scores = jnp.einsum("bqhd,bkhd->bhqk", query, keys, preferred_element_type=jnp.float32) * scale
    probs = jnp.exp(scores - log_total[..., None])
    grad_probs = jnp.einsum(
        "bqhd,bkhd->bhqk", grad_att_heads, values, preferred_element_type=jnp.float32
    )
    grad_scores = (probs * (grad_probs - delta[..., None])).astype(jnp.bfloat16)
    probs, grad_scores = (probs, grad_scores)
    grad_query_rot = (
        jnp.einsum("bhqk,bkhd->bqhd", grad_scores, keys, preferred_element_type=jnp.float32) * scale
    )
    grad_query_raw = (
        rotate(grad_query_rot, cosine, sine, -1.0).reshape(flat, width).astype(jnp.bfloat16)
    )
    grad_key_raw = (
        rotate(grad_keys_acc, cosine, sine, -1.0).reshape(flat, width).astype(jnp.bfloat16)
    )
    grad_value_raw = grad_values_acc.reshape(flat, width).astype(jnp.bfloat16)
    grad_query = matmul(h_one.T, grad_query_raw)
    grad_key = matmul(h_one.T, grad_key_raw)
    grad_value = matmul(h_one.T, grad_value_raw)
    grad_h_one = lax.psum(
        (
            matmul(grad_query_raw, full[1].T)
            + matmul(grad_key_raw, full[2].T)
            + matmul(grad_value_raw, full[3].T)
        ).astype(jnp.bfloat16),
        "tp",
    ).astype(jnp.float32)
    grad_gain_attn = jnp.sum(grad_h_one * normed_one, axis=0)
    grad_tokens = (grad_x_two + norm_back(grad_h_one * gain_one, normed_one, rstd_one)).reshape(
        slots, rows, model
    )
    pieces = (
        lax.psum_scatter(
            grad_gain_attn.astype(jnp.bfloat16), "fsdp", scatter_dimension=0, tiled=True
        ).astype(jnp.float32),
        lax.psum_scatter(
            grad_query.astype(jnp.bfloat16), "fsdp", scatter_dimension=0, tiled=True
        ).astype(jnp.float32),
        lax.psum_scatter(
            grad_key.astype(jnp.bfloat16), "fsdp", scatter_dimension=0, tiled=True
        ).astype(jnp.float32),
        lax.psum_scatter(
            grad_value.astype(jnp.bfloat16), "fsdp", scatter_dimension=0, tiled=True
        ).astype(jnp.float32),
        lax.psum_scatter(
            grad_out.astype(jnp.bfloat16), "fsdp", scatter_dimension=1, tiled=True
        ).astype(jnp.float32),
        lax.psum_scatter(
            grad_gain_ffn.astype(jnp.bfloat16), "fsdp", scatter_dimension=0, tiled=True
        ).astype(jnp.float32),
        lax.psum_scatter(
            grad_gate.astype(jnp.bfloat16), "fsdp", scatter_dimension=0, tiled=True
        ).astype(jnp.float32),
        lax.psum_scatter(
            grad_up.astype(jnp.bfloat16), "fsdp", scatter_dimension=0, tiled=True
        ).astype(jnp.float32),
        lax.psum_scatter(
            grad_down.astype(jnp.bfloat16), "fsdp", scatter_dimension=1, tiled=True
        ).astype(jnp.float32),
    )
    owned = (
        lax.psum(pieces[0].astype(jnp.bfloat16), "ctx").astype(jnp.float32),
        lax.psum(pieces[1].astype(jnp.bfloat16), "ctx").astype(jnp.float32),
        lax.psum(pieces[2].astype(jnp.bfloat16), "ctx").astype(jnp.float32),
        lax.psum(pieces[3].astype(jnp.bfloat16), "ctx").astype(jnp.float32),
        lax.psum(pieces[4].astype(jnp.bfloat16), "ctx").astype(jnp.float32),
        lax.psum(pieces[5].astype(jnp.bfloat16), "ctx").astype(jnp.float32),
        lax.psum(pieces[6].astype(jnp.bfloat16), "ctx").astype(jnp.float32),
        lax.psum(pieces[7].astype(jnp.bfloat16), "ctx").astype(jnp.float32),
        lax.psum(pieces[8].astype(jnp.bfloat16), "ctx").astype(jnp.float32),
    )
    return (
        output,
        grad_tokens,
        owned[0],
        owned[1],
        owned[2],
        owned[3],
        owned[4],
        owned[5],
        owned[6],
        owned[7],
        owned[8],
    )


MESH = pl.DeviceIdType.MESH


def dot(a, b, over):
    return lax.dot_general(a, b, (over, ((), ())), preferred_element_type=jnp.float32)


def turn(u):
    lane = lax.broadcasted_iota(jnp.int32, u.shape, 1)
    return jnp.where(lane % HD < HD // 2, -pltpu.roll(u, 96, 1), pltpu.roll(u, 32, 1))


def rope_tables(rows):
    angle = np.arange(2 * rows, dtype=np.float32)[:, None] * (
        np.float32(1.0)
        / np.float32(rope_base) ** (np.arange(0, HD, 2, dtype=np.float32) / np.float32(HD))
    )[None, :].astype(np.float32)
    tables = []
    for values in (np.cos(angle), np.sin(angle)):
        whole = jnp.asarray(np.tile(values.astype(np.float32), (1, 4)))
        flipped = jnp.concatenate([whole[rows:], whole[:rows]], axis=0)
        tables.append(jnp.where(lax.axis_index("ctx") == 0, whole, flipped))
    return tables


def remote(src, dst, send, recv, to):
    return pltpu.make_async_remote_copy(
        src_ref=src, dst_ref=dst, send_sem=send, recv_sem=recv, device_id=to, device_id_type=MESH
    )


def position():
    f = lax.axis_index("fsdp")
    return f, f // 2, lax.rem(f, 2), lax.axis_index("ctx"), lax.axis_index("tp")


def greet_all(peers):
    barrier = pltpu.get_barrier_semaphore()
    for peer in peers:
        pl.semaphore_signal(barrier, inc=1, device_id=peer, device_id_type=MESH)
    pl.semaphore_wait(barrier, len(peers))


class Gather:
    def __init__(self, buf, send, recv, half):
        f, z, y, c, _ = position()
        rows = buf.shape[1]
        part = pl.ds(0, rows)
        if half:
            part = pl.ds(pl.multiple_of(c * (rows // 2), 16), rows // 2)

        def hop(slot, n, to):
            ref = buf.at[slot, part]
            return remote(ref, ref, send.at[n], recv.at[n], to)

        across = z * 2 + 1 - y
        came = [lax.rem(z + 3 - k, 4) * 2 + y for k in range(3)]
        far = [lax.rem(z + 3 - k, 4) * 2 + 1 - y for k in range(3)]
        over_y, over_x = {"fsdp": across}, {"ctx": 1 - c}
        self.along = [hop(f, k, {"fsdp": lax.rem(z + k + 1, 4) * 2 + y}) for k in range(3)]
        self.own_y = hop(f, 3, over_y)
        self.next_y = [hop(came[k], 4 + k, over_y) for k in range(3)]
        self.half = half
        if half:
            self.own_x = hop(across, 7, over_x)
            self.next_x = [hop(came[k], 8 + k, over_x) for k in range(3)]
            self.last_x = [hop(far[k], 11 + k, over_x) for k in range(3)]

    def begin(self):
        self.along[0].start()
        self.own_y.start()
        self.along[1].start()
        self.along[2].start()

    def middle(self):
        if self.half:
            self.own_y.wait_recv()
            self.own_x.start()
        for k in range(3):
            self.along[k].wait_recv()
            self.next_y[k].start()
            if self.half:
                self.next_x[k].start()

    def late(self):
        if self.half:
            for k in range(3):
                self.next_y[k].wait_recv()
                self.last_x[k].start()

    def ready(self):
        if self.half:
            for copy in [self.own_x] + self.next_x + self.last_x:
                copy.wait_recv()
        else:
            for copy in [self.own_y] + self.next_y:
                copy.wait_recv()

    def finish(self):
        copies = self.along + [self.own_y] + self.next_y
        if self.half:
            copies = copies + [self.own_x] + self.next_x + self.last_x
        for copy in copies:
            copy.wait_send()


class Swap:
    def __init__(self, src, there, here, send, recv):
        _, _, _, c, t = position()
        rows = here.shape[0] // 2
        part = pl.ds(pl.multiple_of(t * rows, 16), rows)
        self.over_x = remote(src.at[part], there.at[part], send.at[0], recv.at[0], {"ctx": 1 - c})
        self.over = remote(here.at[part], here.at[part], send.at[1], recv.at[1], {"tp": 1 - t})

    def begin(self):
        self.over_x.start()

    def middle(self):
        self.over_x.wait_recv()
        self.over.start()

    def ready(self):
        self.over.wait_recv()

    def finish(self):
        self.over_x.wait_send()
        self.over.wait_send()


class TwoCores:
    def __init__(self, own, other, send, recv, chunk):
        t = lax.axis_index("tp")
        self.own, self.other, self.chunk = own, other, chunk
        self.copies = []
        for n in range(own.shape[0] // chunk):
            at = pl.ds(n * chunk, chunk)
            self.copies.append(
                remote(own.at[at], other.at[at], send.at[n], recv.at[n], {"tp": 1 - t})
            )

    def give(self, n, part):
        self.own[n * self.chunk : (n + 1) * self.chunk, :] = part.astype(jnp.bfloat16)
        self.copies[n].start()

    def take(self, n):
        at = slice(n * self.chunk, (n + 1) * self.chunk)
        self.copies[n].wait_recv()
        return self.own[at, :].astype(jnp.float32) + self.other[at, :].astype(jnp.float32)

    def finish(self):
        for copy in self.copies:
            copy.wait_send()


def place_matrix(n, part, model):
    row = lax.broadcasted_iota(jnp.int32, (128, model), 0)
    col = lax.broadcasted_iota(jnp.int32, (128, model), 1)
    return jnp.where((col == row + n * part) & (row < part), 1.0, 0.0)


CHUNK = 256


def forward_kernel(*refs, part, tile):
    tok, cot, gains, wq, wk, wv, wo, wgu, wd, cos_ref, sin_ref = refs[:11]
    outs = refs[11:31]
    (came, cotcame, gbuf, gain, h1, q, k, v, o, lse, x2, h2, hid, upf, act, wqkv, wob, wgub, wdb, y) = refs[31:51]
    pa, oa, pb, ob, gsend, grecv, wsend, wrecv, ssend, srecv, tsend, trecv, osem = refs[51:]
    f, z, yy, c, t = position()
    count = 8
    model = h1.shape[1]
    rows = h1.shape[0]
    half = rows // 2
    width = q.shape[1]
    pairs = width // 128
    units = hid.shape[1]
    chunks = rows // CHUNK

    for p in range(pairs):
        at = slice(p * 128, (p + 1) * 128)
        wqkv[p, f, :, 0:128] = wq[:, at]
        wqkv[p, f, :, 128:256] = wk[:, at]
        wqkv[p, f, :, 256:384] = wv[:, at]
    gbuf[f] = gains[...]
    greet_all(
        [{"fsdp": lax.rem(f + n, count)} for n in range(1, count)]
        + [{"ctx": 1 - c}, {"tp": 1 - t}]
    )
    gain_copies = [
        remote(gbuf.at[f], gbuf.at[f], gsend.at[n - 1], grecv.at[n - 1], {"fsdp": lax.rem(f + n, count)})
        for n in range(1, count)
    ]
    for copy in gain_copies:
        copy.start()
    pieces = []
    for n in range(pairs):
        pieces.append(Gather(wqkv.at[n], wsend.at[n], wrecv.at[n], HALF[n]))
    for n, buf in enumerate((wob, wgub, wdb)):
        n += pairs
        pieces.append(Gather(buf, wsend.at[n], wrecv.at[n], HALF[n]))
    tokens = Swap(tok.at[1 - c], came, came, ssend.at[0], srecv.at[0])
    cotan = Swap(cot.at[1 - c], cotcame, cotcame, ssend.at[1], srecv.at[1])
    a0, a1, a2, b0, b1, b2 = pieces
    a0.begin()
    tokens.begin()
    a1.begin()
    wob[f] = wo[...]
    wgub[f] = wgu[...]
    wdb[f] = wd[...]

    for n in range(half // CHUNK):
        at = slice(n * CHUNK, (n + 1) * CHUNK)
        x2[at, :] = layer_norm(tok[c, at, :].astype(jnp.float32))[0]
    a0.middle()
    a2.begin()
    for copy in gain_copies:
        copy.wait_recv()
    total = jnp.zeros((8, model), jnp.float32)
    for n in range(count):
        total += jnp.dot(gbuf[n], place_matrix(n, part, model), preferred_element_type=jnp.float32)
    gain[...] = total
    gain_one, gain_two = total[0:1], total[1:2]
    for n in range(half // CHUNK):
        at = slice(n * CHUNK, (n + 1) * CHUNK)
        h1[at, :] = (x2[at, :] * gain_one).astype(jnp.bfloat16)
    tokens.middle()
    a0.late()
    a1.middle()
    b0.begin()
    tokens.ready()
    cotan.begin()
    for n in range(half // CHUNK):
        at = slice(n * CHUNK, (n + 1) * CHUNK)
        there = slice(half + n * CHUNK, half + (n + 1) * CHUNK)
        h1[there, :] = (layer_norm(came[at, :].astype(jnp.float32))[0] * gain_one).astype(jnp.bfloat16)
    a0.ready()

    out_copies = []

    def emit(n, ref):
        copy = pltpu.make_async_copy(ref, outs[n], osem.at[n])
        copy.start()
        out_copies.append(copy)

    emit(0, came)
    emit(2, gbuf)
    emit(3, gain)
    emit(4, h1)

    def attend_pair(p, between):
        cols = slice(p * 128, (p + 1) * 128)
        w = wqkv[p].reshape(model, 384)
        lane = lax.broadcasted_iota(jnp.int32, (tile, 128), 1)
        for start in range(0, rows, tile):
            at = slice(start, start + tile)
            raw = jnp.dot(h1[at, :], w, preferred_element_type=jnp.float32)
            cosine, sine = cos_ref[at, :], sin_ref[at, :]
            q_raw, k_raw = raw[:, :128], raw[:, 128:256]
            q[at, cols] = (q_raw * cosine + turn(q_raw) * sine).astype(jnp.bfloat16)
            k[at, cols] = (k_raw * cosine + turn(k_raw) * sine).astype(jnp.bfloat16)
            v[at, cols] = raw[:, 256:].astype(jnp.bfloat16)
        v_turned = v[:, cols].astype(jnp.float32).T.astype(jnp.bfloat16)
        keys = k[:, cols]
        for n, start in enumerate(range(0, rows, tile)):
            at = slice(start, start + tile)
            query = q[at, cols] * jnp.bfloat16(HD ** (-0.5))
            heads = []
            for head in range(2):
                mine = (lane // HD) == head
                qm = jnp.where(mine, query, jnp.zeros_like(query))
                s = dot(keys, qm, ((1,), (1,)))
                top = jnp.max(s, axis=0, keepdims=True)
                e = jnp.exp(s - top)
                total = jnp.sum(e, axis=0, keepdims=True)
                lse[p, head : head + 1, at] = top + jnp.log(total)
                vh = v_turned[head * HD : (head + 1) * HD]
                heads.append(dot(vh, e.astype(jnp.bfloat16), ((1,), (0,))) / total)
            o[at, cols] = jnp.concatenate(heads, axis=0).T.astype(jnp.bfloat16)
            between[n]()

    def after_0():
        a1.late()
        a2.middle()
        b1.begin()

    def after_1():
        a2.late()
        b0.middle()
        cotan.middle()

    attend_pair(0, [after_0, lambda: None])
    a1.ready()
    attend_pair(1, [after_1, lambda: None])
    a2.ready()
    attend_pair(2, [lambda: (b0.late(), b1.middle(), b2.begin()), lambda: None])
    emit(5, q)
    emit(6, k)
    emit(7, v)
    emit(8, o)
    emit(9, lse)
    emit(15, wqkv)

    b0.ready()
    sum_one = TwoCores(pa, oa, tsend.at[0], trecv.at[0], CHUNK)
    sum_two = TwoCores(pb, ob, tsend.at[1], trecv.at[1], CHUNK)
    w = wob[...].reshape(model, width)
    for n in range(chunks):
        sum_one.give(n, dot(o[n * CHUNK : (n + 1) * CHUNK, :], w, ((1,), (1,))))
    b1.late()
    cotan.ready()
    emit(1, cotcame)
    emit(16, wob)
    for n in range(chunks):
        at = slice(n * CHUNK, (n + 1) * CHUNK)
        if n < chunks // 2:
            x = tok[c, at, :]
        else:
            x = came[n * CHUNK - half : (n + 1) * CHUNK - half, :]
        xx = x.astype(jnp.float32) + sum_one.take(n)
        x2[at, :] = xx
        h2[at, :] = (layer_norm(xx)[0] * gain_two).astype(jnp.bfloat16)
    emit(10, x2)
    emit(11, h2)
    b2.middle()
    b1.ready()
    w = wgub[...].reshape(model, 2 * units)
    for n in range(chunks):
        at = slice(n * CHUNK, (n + 1) * CHUNK)
        both = jnp.dot(h2[at, :], w, preferred_element_type=jnp.float32)
        gate, up = both[:, :units], both[:, units:]
        phi = 0.5 + 0.5 * lax.erf(gate * (0.5 ** 0.5))
        active = gate * phi
        slope = phi + gate * (jnp.exp(-0.5 * gate * gate) * (1.0 / (2.0 * np.pi) ** 0.5))
        hid[at, :] = (active * up).astype(jnp.bfloat16)
        upf[at, :] = (slope * up).astype(jnp.bfloat16)
        act[at, :] = active.astype(jnp.bfloat16)
        if n == 0:
            b2.late()
    b2.ready()
    emit(12, hid)
    emit(13, upf)
    emit(14, act)
    emit(17, wgub)
    emit(18, wdb)
    w = wdb[...].reshape(model, units)
    for n in range(chunks):
        sum_two.give(n, dot(hid[n * CHUNK : (n + 1) * CHUNK, :], w, ((1,), (1,))))
    for n in range(chunks):
        at = slice(n * CHUNK, (n + 1) * CHUNK)
        y[at, :] = (x2[at, :] + sum_two.take(n)).astype(jnp.bfloat16)
    emit(19, y)
    for piece in pieces + [tokens, cotan, sum_one, sum_two]:
        piece.finish()
    for copy in gain_copies:
        copy.wait_send()
    for copy in out_copies:
        copy.wait()


HALF = (False, False, True, False, True, True)


def forward(tokens, cotangent, gains, wq, wk, wv, wo, wgu, wd, cosine, sine):
    slots, half, model = tokens.shape
    rows = 2 * half
    part, width = wq.shape
    units = wd.shape[1]
    pairs = width // 128
    low, full = jnp.bfloat16, jnp.float32
    held = [
        ((half, model), low),
        ((half, model), low),
        ((8, 8, 128), full),
        ((8, model), full),
        ((rows, model), low),
        ((rows, width), low),
        ((rows, width), low),
        ((rows, width), low),
        ((rows, width), low),
        ((pairs, 2, rows), full),
        ((rows, model), full),
        ((rows, model), low),
        ((rows, units), low),
        ((rows, units), low),
        ((rows, units), low),
        ((pairs, 8, part, 384), low),
        ((8, part, width), low),
        ((8, part, 2 * units), low),
        ((8, part, units), low),
        ((rows, model), low),
    ]
    dma = pltpu.SemaphoreType.DMA
    return pl.pallas_call(
        partial(forward_kernel, part=part, tile=min(512, rows)),
        in_specs=[pl.BlockSpec(memory_space=pltpu.VMEM)] * 11,
        out_specs=[pl.BlockSpec(memory_space=pl.ANY)] * 20,
        out_shape=[jax.ShapeDtypeStruct(s, d) for s, d in held],
        scratch_shapes=[pltpu.VMEM(s, d) for s, d in held]
        + [pltpu.VMEM((rows, model), low)] * 4
        + [dma((7,)), dma((7,)), dma((6, 14)), dma((6, 14)), dma((2, 2)), dma((2, 2))]
        + [dma((2, rows // CHUNK)), dma((2, rows // CHUNK)), dma((20,))],
        compiler_params=pltpu.CompilerParams(
            collective_id=2, has_side_effects=True, vmem_limit_bytes=56 << 20
        ),
        name="forward",
    )(tokens, cotangent, gains, wq, wk, wv, wo, wgu, wd, cosine, sine)


class Scatter:
    def __init__(self, grad, bufs, send, recv, half):
        f, z, y, c, _ = position()
        self.grad, self.half = grad, half
        self.own = f
        rows = grad.shape[1]
        self.rows = rows
        self.slots = [lax.rem(z + 1 + k, 4) * 2 + y for k in range(4)]
        far = [lax.rem(z + 1 + k, 4) * 2 + 1 - y for k in range(4)]
        over_x, over_y = {"ctx": 1 - c}, {"fsdp": z * 2 + 1 - y}
        if half:
            rows = rows // 2
            self.at = pl.ds(pl.multiple_of(c * rows, 16), rows)
            other = pl.ds(pl.multiple_of((1 - c) * rows, 16), rows)
            self.x_far, self.x_near, self.ry, self.rz, self.low = bufs
            self.first = [
                remote(grad.at[far[k], other], self.x_far.at[k], send.at[8 + k], recv.at[8 + k], over_x)
                for k in range(4)
            ] + [
                remote(grad.at[self.slots[k], other], self.x_near.at[k], send.at[12 + k], recv.at[12 + k], over_x)
                for k in range(4)
            ]
        else:
            self.at = pl.ds(0, rows)
            self.ry, self.rz, self.low, self.rx = bufs
        self.far = far
        self.over_y = [
            remote(grad.at[far[k], self.at], self.ry.at[k], send.at[k], recv.at[k], over_y)
            for k in range(4)
        ]
        self.along = [
            remote(
                grad.at[self.slots[k], self.at], self.rz.at[k], send.at[4 + k], recv.at[4 + k],
                {"fsdp": self.slots[k]},
            )
            for k in range(3)
        ]
        if half:
            part = self.low.at[self.at]
            self.last = remote(part, part, send.at[7], recv.at[7], over_x)
        else:
            self.last = remote(self.low, self.rx, send.at[7], recv.at[7], over_x)

    def begin(self):
        for copy in self.first if self.half else self.over_y:
            copy.start()

    def swap(self):
        if self.half:
            for k in range(4):
                self.first[k].wait_recv()
                block = self.grad[self.far[k], self.at, :].astype(jnp.float32)
                self.grad[self.far[k], self.at, :] = (
                    block + self.x_far[k].astype(jnp.float32)
                ).astype(jnp.bfloat16)
                self.over_y[k].start()

    def middle(self):
        for k in range(4):
            total = self.grad[self.slots[k], self.at, :].astype(jnp.float32)
            if self.half:
                self.first[4 + k].wait_recv()
                total += self.x_near[k].astype(jnp.float32)
            self.over_y[k].wait_recv()
            total += self.ry[k].astype(jnp.float32)
            self.grad[self.slots[k], self.at, :] = total.astype(jnp.bfloat16)
            if k < 3:
                self.along[k].start()

    def late(self):
        total = self.grad[self.own, self.at, :].astype(jnp.float32)
        for k in range(3):
            self.along[k].wait_recv()
            total += self.rz[k].astype(jnp.float32)
        self.low[self.at, :] = total.astype(jnp.bfloat16)
        self.last.start()

    def result(self):
        self.last.wait_recv()
        total = self.low[...].astype(jnp.float32)
        if not self.half:
            total += self.rx[...].astype(jnp.float32)
        return total

    def finish(self):
        for copy in self.over_y + self.along + [self.last] + (self.first if self.half else []):
            copy.wait_send()


def scatter_buffers(part, cols, half):
    low = jnp.bfloat16
    if half:
        rows = part // 2
        return [pltpu.VMEM((4, rows, cols), low)] * 3 + [
            pltpu.VMEM((3, rows, cols), low),
            pltpu.VMEM((part, cols), low),
        ]
    return [
        pltpu.VMEM((4, part, cols), low),
        pltpu.VMEM((3, part, cols), low),
        pltpu.VMEM((part, cols), low),
        pltpu.VMEM((part, cols), low),
    ]


SUM_HALF = (False, True, False, False, False, False)


def norm_back_of(grad, gain, normed, rstd):
    return norm_back(grad * gain, normed, rstd)


def backward_kernel(*refs, part, tile, bounds):
    ins = refs[: bounds[0]]
    (output, grad_tokens, g_q, g_k, g_v, g_out, g_gate, g_up, g_down, g_gains) = refs[bounds[0] : bounds[1]]
    (g, x, gain, q, k, v, o, lse, h1, x2, h2, hid, upf, act, wqkv, wob, wgub, wdb, cos_ref, sin_ref) = refs[
        bounds[1] : bounds[2]
    ]
    (gb, ab, do, dqkv, dk_ref, dv_ref, pa, oa, pb, ob, low, lowcame, ggs, gga, ggr, ggx, ggl) = refs[bounds[2] : bounds[3]]
    gd, gu, go, gp = refs[bounds[3] : bounds[3] + 4]
    rest = list(refs[bounds[3] + 4 :])
    lsem, send, recv, ssend, srecv, tsend, trecv, gsend, grecv, gxsem, esem = rest[-11:]
    bufs = rest[:-11]
    (tok, came, cot, cotcame, gain_in, q_in, k_in, v_in, o_in, lse_in, h1_in, x2_in, h2_in, hid_in, up_in, act_in,
     wqkv_in, wo_in, wgu_in, wd_in, y, cos_in, sin_in) = ins
    f, z, yy, c, t = position()
    count = 8
    rows, model = h1.shape
    half = rows // 2
    width = q.shape[1]
    pairs = width // 128
    units = hid.shape[1]
    chunks = rows // CHUNK
    top_half, low_half = pl.ds(0, half), pl.ds(half, half)

    loads = []

    def load(src, dst):
        copy = pltpu.make_async_copy(src, dst, lsem.at[len(loads)])
        copy.start()
        loads.append(copy)
        return copy

    need_g = [load(cot.at[c], g.at[top_half]), load(cotcame, g.at[low_half])]
    need_one = [load(wd_in, wdb), load(up_in, upf), load(act_in, act)]
    need_two = [load(wgu_in, wgub)]
    need_three = [load(hid_in, hid), load(h2_in, h2)]
    need_four = [load(x2_in, x2), load(gain_in, gain)]
    need_five = [load(wo_in, wob), load(o_in, o)]
    need_six = [load(q_in, q), load(k_in, k), load(v_in, v), load(lse_in, lse), load(cos_in, cos_ref), load(sin_in, sin_ref)]
    need_seven = [load(h1_in, h1), load(wqkv_in, wqkv)]
    need_eight = [load(tok.at[c], x.at[top_half]), load(came, x.at[low_half])]

    def need(copies):
        for copy in copies:
            copy.wait()

    greet_all(
        [{"fsdp": lax.rem(f + n, count)} for n in range(1, count)]
        + [{"ctx": 1 - c}, {"tp": 1 - t}]
    )
    grads = [gd, gu, go] + [gp.at[n] for n in range(pairs)]
    sums = []
    for n, grad in enumerate(grads):
        many = 5 if SUM_HALF[n] else 4
        sums.append(Scatter(grad, bufs[:many], send.at[n], recv.at[n], SUM_HALF[n]))
        bufs = bufs[many:]
    s_down, s_ffn, s_out, s_0, s_1, s_2 = sums
    sum_one = TwoCores(pa, oa, tsend.at[0], trecv.at[0], CHUNK)
    sum_two = TwoCores(pb, ob, tsend.at[1], trecv.at[1], CHUNK)

    swap_out = Swap(y.at[low_half], output.at[c], output.at[1 - c], ssend.at[0], srecv.at[0])
    swap_out.begin()
    kept = pltpu.make_async_copy(y.at[top_half], output.at[c], esem.at[0])
    kept.start()

    need(need_g)
    need(need_one)
    w = wdb[...].reshape(model, units)
    for n in range(chunks):
        at = slice(n * CHUNK, (n + 1) * CHUNK)
        dh = jnp.dot(g[at, :], w, preferred_element_type=jnp.float32)
        gb[at, :units] = (dh * upf[at, :].astype(jnp.float32)).astype(jnp.bfloat16)
        gb[at, units:] = (dh * act[at, :].astype(jnp.float32)).astype(jnp.bfloat16)
    need(need_two)
    w = wgub[...].reshape(model, 2 * units)
    for n in range(chunks):
        sum_one.give(n, dot(gb[n * CHUNK : (n + 1) * CHUNK, :], w, ((1,), (1,))))
    need(need_three)

    def weight_grad(into, left, right):
        for n in range(2):
            cols = slice(n * (model // 2), (n + 1) * (model // 2))
            block = dot(left[:, cols], right, ((0,), (0,)))
            into[n * 4 : (n + 1) * 4, :, :] = block.astype(jnp.bfloat16).reshape(4, part, -1)

    weight_grad(gu, h2, gb[...])
    s_ffn.begin()
    weight_grad(gd, g, hid[...])
    s_down.begin()
    need(need_four)
    gain_one, gain_two = gain[0:1, :], gain[1:2, :]
    total = jnp.zeros((1, model), jnp.float32)
    for n in range(chunks):
        at = slice(n * CHUNK, (n + 1) * CHUNK)
        dh2 = sum_one.take(n)
        normed, rstd = layer_norm(x2[at, :])
        total += jnp.sum(dh2 * normed, axis=0, keepdims=True)
        dx2 = g[at, :].astype(jnp.float32) + norm_back_of(dh2, gain_two, normed, rstd)
        x2[at, :] = dx2
        ab[at, :] = dx2.astype(jnp.bfloat16)
    gga[...] = jnp.zeros_like(gga)
    gga[1:2, :] = total
    s_ffn.swap()
    swap_out.middle()
    need(need_five)
    w = wob[...].reshape(model, width)
    for n in range(chunks):
        at = slice(n * CHUNK, (n + 1) * CHUNK)
        do[at, :] = jnp.dot(ab[at, :], w, preferred_element_type=jnp.float32).astype(jnp.bfloat16)
    weight_grad(go, ab, o[...])
    s_down.middle()
    s_out.begin()
    need(need_six)

    def attend_back_pair(p, between):
        cols = slice(p * 128, (p + 1) * 128)
        keys, values = k[:, cols], v[:, cols]
        k_turned = keys.astype(jnp.float32).T.astype(jnp.bfloat16)
        lane = lax.broadcasted_iota(jnp.int32, (tile, 128), 1)
        dk_ref[...] = jnp.zeros_like(dk_ref)
        dv_ref[...] = jnp.zeros_like(dv_ref)
        for n, start in enumerate(range(0, rows, tile)):
            at = slice(start, start + tile)
            query = q[at, cols] * jnp.bfloat16(HD ** (-0.5))
            grad = do[at, cols]
            prod = (grad.astype(jnp.float32) * o[at, cols].astype(jnp.float32)).T
            heads = []
            for head in range(2):
                mine = (lane // HD) == head
                qm = jnp.where(mine, query, jnp.zeros_like(query))
                dm = jnp.where(mine, grad, jnp.zeros_like(grad))
                delta = jnp.sum(prod[head * HD : (head + 1) * HD], axis=0, keepdims=True)
                pr = jnp.exp(dot(keys, qm, ((1,), (1,))) - lse[p, head : head + 1, at])
                ds = (pr * (dot(values, dm, ((1,), (1,))) - delta)).astype(jnp.bfloat16)
                dv_ref[...] += dot(pr.astype(jnp.bfloat16), dm, ((1,), (0,)))
                dk_ref[...] += dot(ds, qm, ((1,), (0,)))
                heads.append(dot(k_turned[head * HD : (head + 1) * HD], ds, ((1,), (0,))))
            dq = jnp.concatenate(heads, axis=0).T * (HD ** (-0.5))
            dq = dq * cos_ref[at, :] - turn(dq) * sin_ref[at, :]
            dqkv[at, p * 384 : p * 384 + 128] = dq.astype(jnp.bfloat16)
            between[n]()
        dk = dk_ref[...]
        dk = dk * cos_ref[...] - turn(dk) * sin_ref[...]
        dqkv[:, p * 384 + 128 : p * 384 + 256] = dk.astype(jnp.bfloat16)
        dqkv[:, p * 384 + 256 : p * 384 + 384] = dv_ref[...].astype(jnp.bfloat16)

    attend_back_pair(0, [lambda: s_ffn.middle(), lambda: (s_down.late(), s_out.middle())])
    need(need_seven)
    weight_grad(gp.at[0], h1, dqkv[:, 0:384])
    s_0.begin()
    attend_back_pair(1, [lambda: s_ffn.late(), lambda: (s_out.late(), s_0.middle())])
    weight_grad(gp.at[1], h1, dqkv[:, 384:768])
    s_1.begin()
    swap_out.ready()
    g_down[...] = s_down.result().T
    attend_back_pair(2, [lambda: None, lambda: (s_0.late(), s_1.middle())])
    weight_grad(gp.at[2], h1, dqkv[:, 768:1152])
    s_2.begin()

    order = list(range(chunks // 2, chunks)) + list(range(chunks // 2))
    for n in order:
        at = slice(n * CHUNK, (n + 1) * CHUNK)
        total = jnp.zeros((CHUNK, model), jnp.float32)
        for p in range(pairs):
            total += dot(dqkv[at, p * 384 : (p + 1) * 384], wqkv[p].reshape(model, 384), ((1,), (1,)))
        sum_two.give(n, total)
    need(need_eight)
    swap_x = Swap(low, lowcame, lowcame, ssend.at[1], srecv.at[1])
    total = jnp.zeros((1, model), jnp.float32)
    stores = []
    for i, n in enumerate(order):
        at = slice(n * CHUNK, (n + 1) * CHUNK)
        dh1 = sum_two.take(n)
        normed, rstd = layer_norm(x[at, :].astype(jnp.float32))
        total += jnp.sum(dh1 * normed, axis=0, keepdims=True)
        dx = x2[at, :] + norm_back_of(dh1, gain_one, normed, rstd)
        if n >= chunks // 2:
            low[n * CHUNK - half : (n + 1) * CHUNK - half, :] = dx.astype(jnp.bfloat16)
        else:
            x2[at, :] = dx
        if i == chunks // 2 - 1:
            swap_x.begin()
            s_1.late()
            s_2.middle()
    gga[0:1, :] = total
    for n in range(count):
        turned = place_matrix(n, part, model)
        ggs[n] = dot(gga[...], turned, ((1,), (1,)))
    to_owner = [
        remote(ggs.at[lax.rem(f + n, count)], ggr.at[n], gsend.at[n - 1], grecv.at[n - 1], {"fsdp": lax.rem(f + n, count)})
        for n in range(1, count)
    ]
    for copy in to_owner:
        copy.start()
    stores.append(pltpu.make_async_copy(x2.at[top_half], grad_tokens.at[c], esem.at[1]))
    stores[-1].start()
    swap_x.middle()
    total = ggs[f]
    for n in range(1, count):
        to_owner[n - 1].wait_recv()
        total += ggr[n]
    ggl[...] = total
    ggcopy = remote(ggl, ggx, gxsem.at[0], gxsem.at[1], {"ctx": 1 - c})
    ggcopy.start()
    both = s_ffn.result()
    g_gate[...] = both[:, :units]
    g_up[...] = both[:, units:]
    g_out[...] = s_out.result().T
    s_2.late()
    swap_x.ready()
    x2[half:, :] = lowcame[...].astype(jnp.float32)
    stores.append(pltpu.make_async_copy(x2.at[low_half], grad_tokens.at[1 - c], esem.at[2]))
    stores[-1].start()
    for p, piece in enumerate((s_0, s_1, s_2)):
        block = piece.result()
        at = slice(p * 128, (p + 1) * 128)
        g_q[:, at] = block[:, 0:128]
        g_k[:, at] = block[:, 128:256]
        g_v[:, at] = block[:, 256:384]
    ggcopy.wait_recv()
    g_gains[...] = ggl[...] + ggx[...]
    ggcopy.wait_send()
    for copy in to_owner:
        copy.wait_send()
    for piece in sums + [sum_one, sum_two, swap_out, swap_x]:
        piece.finish()
    kept.wait()
    for copy in stores:
        copy.wait()


def backward(tokens, came, cotangent, cotcame, gain, h1, q, k, v, o, lse, x2, h2, hid, upf, act, wqkv, wo, wgu, wd, y, cosine, sine):
    slots, half, model = tokens.shape
    rows = 2 * half
    part, width = wo.shape[1:]
    units = wd.shape[2]
    pairs = width // 128
    low, full = jnp.bfloat16, jnp.float32
    ins = (tokens, came, cotangent, cotcame, gain, q, k, v, o, lse, h1, x2, h2, hid, upf, act, wqkv, wo, wgu, wd, y, cosine, sine)
    vm = pltpu.VMEM
    held = [vm((rows, model), low)] * 2 + [
        vm(a.shape, a.dtype)
        for a in (gain, q, k, v, o, lse, h1, x2, h2, hid, upf, act, wqkv, wo, wgu, wd, cosine, sine)
    ]
    work = [
        vm((rows, 2 * units), low),
        vm((rows, model), low),
        vm((rows, width), low),
        vm((rows, 3 * width), low),
        vm((rows, 128), full),
        vm((rows, 128), full),
    ] + [vm((rows, model), low)] * 4 + [
        vm((half, model), low),
        vm((half, model), low),
        vm((8, 8, 128), full),
        vm((8, model), full),
        vm((8, 8, 128), full),
        vm((8, 128), full),
        vm((8, 128), full),
    ]
    grads = [vm((8, part, units), low), vm((8, part, 2 * units), low), vm((8, part, width), low), vm((pairs, 8, part, 384), low)]
    bufs = []
    for cols, halved in zip((units, 2 * units, width, 384, 384, 384), SUM_HALF):
        bufs += scatter_buffers(part, cols, halved)
    dma = pltpu.SemaphoreType.DMA
    sems = [dma((24,)), dma((6, 16)), dma((6, 16)), dma((2, 2)), dma((2, 2))] + [
        dma((2, rows // CHUNK)), dma((2, rows // CHUNK)), dma((7,)), dma((7,)), dma((2,)), dma((3,))
    ]
    small = [(part, width)] * 3 + [(width, part)] + [(part, units)] * 2 + [(units, part), (8, 128)]
    anywhere = pl.BlockSpec(memory_space=pl.ANY)
    first = len(ins)
    second = first + 2 + len(small)
    third = second + len(held)
    fourth = third + len(work)
    return pl.pallas_call(
        partial(backward_kernel, part=part, tile=min(512, rows), bounds=(first, second, third, fourth)),
        in_specs=[anywhere] * len(ins),
        out_specs=[anywhere] * 2 + [pl.BlockSpec(memory_space=pltpu.VMEM)] * len(small),
        out_shape=[jax.ShapeDtypeStruct(tokens.shape, low), jax.ShapeDtypeStruct(tokens.shape, full)]
        + [jax.ShapeDtypeStruct(s, full) for s in small],
        scratch_shapes=held + work + grads + bufs + sems,
        compiler_params=pltpu.CompilerParams(
            collective_id=3, has_side_effects=True, vmem_limit_bytes=60 << 20
        ),
        name="backward",
    )(*ins)


def on_device(
    tokens, gain_attn, w_query, w_key, w_value, w_out, gain_ffn, w_gate, w_up, w_down, cotangent
):
    slots, rows, model = tokens.shape
    part = w_query.shape[0]
    gains = jnp.pad(
        jnp.stack([gain_attn, gain_ffn]).astype(jnp.float32), ((0, 6), (0, 128 - part))
    )
    cosine, sine = rope_tables(rows)
    came, cotcame, _, *kept = forward(
        tokens, cotangent, gains, w_query, w_key, w_value, w_out.T,
        jnp.concatenate([w_gate, w_up], axis=1), w_down.T, cosine, sine,
    )
    (output, grad_tokens, g_query, g_key, g_value, g_out, g_gate, g_up, g_down, own_gains) = backward(
        tokens, came, cotangent, cotcame, *kept, cosine, sine
    )
    return (
        output,
        grad_tokens,
        own_gains[0, :part],
        g_query,
        g_key,
        g_value,
        g_out,
        own_gains[1, :part],
        g_gate,
        g_up,
        g_down,
    )


def solution(mesh):
    whole = mesh.shape["ctx"] == 2 and mesh.shape["tp"] == 2
    step = on_device if whole and mesh.shape["fsdp"] == 8 else on_device_blocks
    placed = (
        P(None, ("fsdp", "ctx"), None),
        P("fsdp"),
        P("fsdp", "tp"),
        P("fsdp", "tp"),
        P("fsdp", "tp"),
        P("tp", "fsdp"),
        P("fsdp"),
        P("fsdp", "tp"),
        P("fsdp", "tp"),
        P("tp", "fsdp"),
        P(None, ("fsdp", "ctx"), None),
    )
    return jax.shard_map(
        step,
        mesh=mesh,
        in_specs=placed,
        out_specs=(
            P(None, ("fsdp", "ctx"), None),
            P(None, ("fsdp", "ctx"), None),
            P("fsdp"),
            P("fsdp", "tp"),
            P("fsdp", "tp"),
            P("fsdp", "tp"),
            P("tp", "fsdp"),
            P("fsdp"),
            P("fsdp", "tp"),
            P("fsdp", "tp"),
            P("tp", "fsdp"),
        ),
        check_vma=False,
    )
```
